128 devices in a mesh: role: 16 (over z, y_hi, core), tp: 8 (over y_lo, x).
Axes of the slice: x: 4, y: 4 (y_hi: 2, y_lo: 2; y = y_hi * 2 + y_lo), z: 4, core: 2. Of those that a mesh axis runs over, the one named last changes fastest.
Arguments:
- x_pre: bfloat16 [22528, 8192], P('role'), may hold values from -6 to 6
- ln_gain: bfloat16 [8192], replicated, may hold values from 0.25 to 1.75
- w_kv: bfloat16 [8192, 2048], P('role', 'tp'), may hold values from -0.0625 to 0.0625
- kv_bias: bfloat16 [2048], P('tp'), may hold values from -3 to 3
- page_owner: int32 [176, 1], P('role'), may hold values from 0 to 15; in each aligned block of 11 rows (0 to 10, 11 to 21, ...) at most 2 rows name the same one
- page_req: int32 [176], P('role'), may hold values from 0 to 31
- kv_pool: bfloat16 [512, 128, 2048], P('role', None, 'tp'), may hold values from -6 to 6
- block_table: int32 [512, 4], P('role'), may hold values from 0 to 31
- cache_len: int32 [512], P('role'), may hold values from 1 to 512, 131072 in all
- dec_q: bfloat16 [4, 512, 8192], P(None, 'role', 'tp'), may hold values from -100 to 100
- dec_kv: bfloat16 [4, 512, 2048], P(None, 'role', 'tp'), may hold values from -6 to 6
- w_out: bfloat16 [8192, 8192], P('tp', 'role'), may hold values from -0.0625 to 0.0625
Outputs:
- decoded: bfloat16 [4, 512, 8192], P(None, 'tp', 'role')
The draws below stay inside these ranges and needn't reach their ends.
Inputs may be any that keep to these rules, and one draw needn't show every extreme that they name: `page_owner`: of the 11 pages of one role index, at most 2 belong to requests of one owner, and this bound is reached.
All inputs are finite; a program needn't handle non-finite values. No bound on the sum of `cache_len` on one device may be relied on, other than what follows from the above.
Results may differ from the reference program's by a relative error of at most 0.0054.
Values may be sent and summed in bfloat16 or wider, within the bound.
A program may use at most 128 MiB of HBM per device.

```python
import math
import jax
import jax.numpy as jnp
import numpy as np
from jax import lax

D = 8192
QH = 64
KVH = 8
HS = 128
PAGE = 128
CAP = 2
STEPS = 4
MAXP = 4
REQ_DEV = 32
PG_DEV = 11
POOL_DEV = 32
POOL_ALL = 512
REQ = 512
NPAGES = 176
PTOK = 22528
N_ROLE = 16


def draw_dec_kv(key, part):
    key = jax.random.fold_in(key, 1)
    values = jnp.clip(jax.random.normal(key, (STEPS, REQ, KVH, 2, HS), jnp.float32), -6.0, 6.0)
    return values.reshape(STEPS, REQ, KVH * 2 * HS).astype(jnp.bfloat16)


def draw_dec_q(key, part):
    key = jax.random.fold_in(key, 2)
    queries = jnp.clip(jax.random.normal(key, (STEPS, REQ, KVH, QH // KVH, HS), jnp.float32), -6.0, 6.0)
    return queries.reshape(STEPS, REQ, QH * HS).astype(jnp.bfloat16)


def touch_ends(drawn, own_key, low, high):
    longest = drawn.shape.index(max(drawn.shape))
    spots = []
    for shift in (0, 1):
        where = [jax.random.randint(jax.random.fold_in(own_key, axis), (), 0, length) for axis, length in enumerate(drawn.shape)]
        where[longest] = (where[longest] + shift) % drawn.shape[longest]
        spots.append(tuple(where))
    return drawn.at[spots[0]].set(low).at[spots[1]].set(high)


def levels(own_key, shape, pieces, smallest, top_value):
    gain, own = 1.0, jax.random.fold_in(own_key, 6)
    for position, blocks in pieces:
        draws = jnp.exp(jax.random.uniform(jax.random.fold_in(own, position), (blocks,), jnp.float32, smallest / len(pieces), top_value / len(pieces)))
        gain = gain * jnp.repeat(draws, shape[position] // blocks).reshape([-1 if axis == position else 1 for axis in range(len(shape))])
    return gain


def length_profile(amount, total, reach, lean):
    weights = [(1 << 20) // math.isqrt(standing ** lean) + 1 for standing in range(2, amount + 1)]
    rest, holding = total - reach - (amount - 1), [1] * (amount - 1)
    while rest > 0:
        movable = [i for i in range(amount - 1) if holding[i] < reach]
        mass, remaining = sum([weights[i] for i in movable]), rest
        for i in movable:
            more = min(reach - holding[i], max(1, remaining * weights[i] // mass), rest)
            holding[i] = holding[i] + more
            rest = rest - more
    return np.array([reach] + holding)


def ragged_sizes(own_key, count, total, bound, lean):
    if count == 2:
        one = jax.random.randint(own_key, (), max(1, total - bound), min(bound, total - 1) + 1)
        return jnp.stack([one, total - one])
    tallies = jnp.asarray(length_profile(count, total, bound, lean), jnp.int32)
    twos = (count - 1) // 2
    donor, taker = tallies[1:1 + 2 * twos:2], tallies[2:2 + 2 * twos:2]
    slack = jnp.minimum(donor - 1, bound - taker)
    moved = jax.random.randint(jax.random.fold_in(own_key, 1), (twos,), 0, 1 << 20) % (slack + 1)
    tallies = tallies.at[1:1 + 2 * twos:2].set(donor - moved).at[2:2 + 2 * twos:2].set(taker + moved)
    return tallies[jax.random.permutation(jax.random.fold_in(own_key, 2), count)]


def deal_out(key, own, number, rows, amount, top, reach, slope):
    order = jax.random.permutation(key, amount)
    packed, usual = portions_of(amount, rows * top, reach, slope, True), portions_of(amount, rows * top, reach, slope, False)
    places = jnp.arange(amount)

    def named(tallies, turn):
        used = int((tallies > 0).sum())
        fixed = max(1, used // 4)
        moved = fixed + (places - fixed + turn * (used - fixed)) % max(1, amount - fixed)
        return jnp.zeros((amount,), jnp.int32).at[order[jnp.where(places < fixed, places, moved)]].set(jnp.asarray(tallies, jnp.int32))

    tallies = jnp.where(number % 4 == 0, named(packed, number // 4), named(usual, number - number // 4 - 1))
    mixed = jax.random.permutation(jax.random.fold_in(own, 3), amount)
    source_of, sink = mixed[0:amount // 2 * 2:2], mixed[1:amount // 2 * 2:2]
    slack = jnp.minimum(tallies[source_of] - 1, reach - tallies[sink]) // 2
    slack = jnp.where((source_of == order[0]) | (sink == order[0]) | (tallies[sink] == 0), 0, jnp.maximum(slack, 0))
    moved = jax.random.randint(jax.random.fold_in(own, 4), (amount // 2,), 0, 1 << 20) % (slack + 1)
    tallies = tallies.at[source_of].add(-moved).at[sink].add(moved)
    members = jnp.searchsorted(jnp.cumsum(tallies), jnp.arange(rows * top), side="right").astype(jnp.int32)
    grid = members.reshape(top, rows).T
    grid = grid[jax.random.permutation(jax.random.fold_in(own, 1), rows)]
    turn = jax.random.randint(jax.random.fold_in(own, 2), (rows, 1), 0, top)
    return jnp.take_along_axis(grid, (jnp.arange(top)[None, :] + turn) % top, axis=1)


def portions_of(number_of, total, most, lean, full):
    loads = [(1 << 20) // math.isqrt(grade ** lean) + 1 for grade in range(1, number_of + 1)]
    largest = most if full else min(most, max(-(-total // number_of), total * loads[0] // sum(loads)))
    least = 1 if total - largest >= number_of - 1 else 0
    holding, spare = [largest] + [least] * (number_of - 1), total - largest - least * (number_of - 1)
    while spare > 0:
        candidates = [i for i in range(1, number_of) if holding[i] < largest] or [i for i in range(1, number_of) if holding[i] < most]
        pool, budget = sum([loads[i] for i in candidates]), spare
        for i in candidates:
            addition = min(most - holding[i], max(1, budget * loads[i] // pool), spare)
            holding[i] = holding[i] + addition
            spare = spare - addition
    return np.array(holding)


def scatter_about(key, dims, scale, bound, shards=(), held_as=jnp.bfloat16):
    array = scale * jax.random.normal(key, dims, jnp.float32)
    if shards:
        array = array * levels(key, dims, shards, -0.22, 0.18)
    return jnp.clip(array, -bound, bound).astype(held_as)


def setup_inputs(seed: int = 0) -> dict:
    arg_keys = jax.random.split(jax.random.key(seed), 13)
    x_pre = scatter_about(arg_keys[0], (PTOK, D), 1.0, 6.0, ((0, 16),))
    ln_gain = jnp.clip(1.0 + 0.15 * jax.random.normal(arg_keys[1], (D,), jnp.float32), 0.25, 1.75).astype(jnp.bfloat16)
    w_kv = scatter_about(arg_keys[2], (D, 2 * KVH * HS), D ** -0.5, 0.0625, ((0, 16), (1, 8)))
    kv_bias = scatter_about(arg_keys[3], (2 * KVH * HS,), 0.5, 3.0, ((0, 8),))
    page_owner_keys = jax.random.split(jax.random.fold_in(arg_keys[4], 1), NPAGES // PG_DEV)
    page_owner_turns = jax.random.permutation(jax.random.fold_in(arg_keys[4], 3), NPAGES // PG_DEV)
    page_owner = jax.vmap(lambda own, number: deal_out(jax.random.fold_in(arg_keys[4], 2), own, number, PG_DEV, N_ROLE, 1, CAP, 2))(page_owner_keys, page_owner_turns).reshape((NPAGES, 1))
    page_req = touch_ends(jax.random.randint(arg_keys[5], (NPAGES,), 0, REQ_DEV), jax.random.fold_in(arg_keys[5], 1), 0, REQ_DEV - 1).astype(jnp.int32)
    kv_pool = scatter_about(arg_keys[6], (POOL_ALL, PAGE, 2 * KVH * HS), 1.0, 6.0, ((0, 16), (2, 8)))
    block_table = touch_ends(jax.random.randint(arg_keys[7], (REQ, MAXP), 0, POOL_DEV), jax.random.fold_in(arg_keys[7], 1), 0, POOL_DEV - 1).astype(jnp.int32)
    cache_len = ragged_sizes(arg_keys[8], REQ, REQ * PAGE * MAXP // 2, MAXP * PAGE, 1).astype(jnp.int32)
    dec_q = draw_dec_q(jax.random.fold_in(arg_keys[12], 71), 0)
    dec_kv = draw_dec_kv(jax.random.fold_in(arg_keys[12], 71), 0)
    w_out = scatter_about(arg_keys[11], (QH * HS, D), (QH * HS) ** -0.5, 0.0625, ((0, 8), (1, 16)))
    return dict(x_pre=x_pre, ln_gain=ln_gain, w_kv=w_kv, kv_bias=kv_bias, page_owner=page_owner, page_req=page_req, kv_pool=kv_pool, block_table=block_table, cache_len=cache_len, dec_q=dec_q, dec_kv=dec_kv, w_out=w_out)


EPSILON = 1e-06

def reference(x_pre, ln_gain, w_kv, kv_bias, page_owner, page_req, kv_pool, block_table, cache_len, dec_q, dec_kv, w_out):
    per_kv = QH // KVH
    rows_q = STEPS * per_kv
    scaling = 1.0 / math.sqrt(HS)
    activations = x_pre.astype(jnp.float32)
    inverse = lax.rsqrt(lax.optimization_barrier(jnp.mean(activations * activations, axis=-1, keepdims=True)) + EPSILON)
    normed = (activations * inverse * ln_gain.astype(jnp.float32)).astype(jnp.bfloat16)
    fresh_kv = (jnp.dot(normed, w_kv, preferred_element_type=jnp.float32) + kv_bias.astype(jnp.float32)).astype(jnp.bfloat16)
    page_blocks = fresh_kv.reshape(NPAGES, PAGE, KVH, 2, HS).astype(jnp.float32)
    request_of = (page_owner[:, 0] * REQ_DEV + page_req).astype(jnp.int32)
    queries = dec_q.reshape(STEPS, REQ, KVH, per_kv, HS).transpose(1, 2, 0, 3, 4).reshape(REQ, KVH, rows_q, HS).astype(jnp.float32)
    page_queries = queries[request_of]
    page_scores = jnp.einsum('pgqd,ptgd->pgqt', page_queries, page_blocks[:, :, :, 0]) * scaling
    page_top = jax.ops.segment_max(lax.optimization_barrier(jnp.max(page_scores, axis=-1)), request_of, num_segments=REQ)
    own_kv = dec_kv.reshape(STEPS, REQ, KVH, 2, HS).astype(jnp.float32)
    row_step = jnp.arange(rows_q) // per_kv
    causal = jnp.arange(STEPS)[None, :] <= row_step[:, None]
    positions = jnp.arange(MAXP * PAGE)

    def one_group(group_index):
        first = group_index * REQ_DEV
        group_queries = lax.dynamic_slice_in_dim(queries, first, REQ_DEV, 0)
        group_table = lax.dynamic_slice_in_dim(block_table, first, REQ_DEV, 0) + group_index * POOL_DEV
        group_len = lax.dynamic_slice_in_dim(cache_len, first, REQ_DEV, 0)
        group_own = lax.dynamic_slice_in_dim(own_kv, first, REQ_DEV, 1)
        group_page_top = lax.dynamic_slice_in_dim(page_top, first, REQ_DEV, 0)
        cache_kv = kv_pool[group_table].reshape(REQ_DEV, MAXP * PAGE, KVH, 2, HS).astype(jnp.float32)
        is_live = positions[None, :] < group_len[:, None]
        cache_scores = jnp.einsum('rgqd,rtgd->rgqt', group_queries, cache_kv[:, :, :, 0]) * scaling
        cache_scores = jnp.where(is_live[:, None, None, :], cache_scores, -jnp.inf)
        own_scores = jnp.einsum('rgqd,srgd->rgqs', group_queries, group_own[:, :, :, 0]) * scaling
        own_scores = jnp.where(causal[None, None], own_scores, -jnp.inf)
        row_top = jnp.maximum(jnp.maximum(lax.optimization_barrier(jnp.max(cache_scores, axis=-1)), lax.optimization_barrier(jnp.max(own_scores, axis=-1))), group_page_top)
        cache_weights = jnp.where(is_live[:, None, None, :], jnp.exp(cache_scores - row_top[..., None]), 0.0)
        own_weights = jnp.where(causal[None, None], jnp.exp(own_scores - row_top[..., None]), 0.0)
        weight_sum = lax.optimization_barrier(jnp.sum(cache_weights, axis=-1)) + lax.optimization_barrier(jnp.sum(own_weights, axis=-1))
        cache_probs = lax.optimization_barrier(cache_weights.astype(jnp.bfloat16)).astype(jnp.float32)
        own_probs = lax.optimization_barrier(own_weights.astype(jnp.bfloat16)).astype(jnp.float32)
        accumulated = jnp.einsum('rgqt,rtgd->rgqd', cache_probs, cache_kv[:, :, :, 1])
        accumulated = accumulated + jnp.einsum('rgqs,srgd->rgqd', own_probs, group_own[:, :, :, 1])
        return (row_top, weight_sum, accumulated)
    row_top, weight_sum, accumulated = lax.map(one_group, jnp.arange(N_ROLE))
    row_top = row_top.reshape(REQ, KVH, rows_q)
    weight_sum = weight_sum.reshape(REQ, KVH, rows_q)
    accumulated = accumulated.reshape(REQ, KVH, rows_q, HS)
    page_weights = jnp.exp(page_scores - row_top[request_of][..., None])
    weight_sum = weight_sum + jax.ops.segment_sum(lax.optimization_barrier(jnp.sum(page_weights, axis=-1)), request_of, num_segments=REQ)
    page_probs = lax.optimization_barrier(page_weights.astype(jnp.bfloat16)).astype(jnp.float32)
    page_terms = jnp.einsum('pgqt,ptgd->pgqd', page_probs, page_blocks[:, :, :, 1])
    accumulated = accumulated + jax.ops.segment_sum(page_terms, request_of, num_segments=REQ)
    attention = accumulated / weight_sum[..., None]
    attention = attention.reshape(REQ, KVH, STEPS, per_kv, HS).transpose(2, 0, 1, 3, 4).reshape(STEPS * REQ, QH * HS).astype(jnp.bfloat16)
    decoded = jnp.dot(attention, w_out, preferred_element_type=jnp.float32).astype(jnp.bfloat16)
    return decoded.reshape(STEPS, REQ, D)
```

```python
import functools
import math

import jax
import jax.numpy as jnp
from jax import lax
from jax.experimental import pallas as pl
from jax.experimental.pallas import tpu as pltpu
from jax.sharding import PartitionSpec as P

HS = 128
PAGE = 128
EPSILON = 1e-06
LOW = -1e30
MESH = pl.DeviceIdType.MESH
BF = jnp.bfloat16
F32 = jnp.float32

NR = 16
NT = 8
NP = 11
RQ = 32
STEPS = 4
PER = 8
KB = 512
KVW = 256
ROWS = NP * PAGE
TILE = 352
NOUT = 512
SCALING = 1.0 / math.sqrt(HS)
NT_DIMS = (((1,), (1,)), ((), ()))


def kernel(
    x_hbm,
    w_hbm,
    bias_ref,
    owner_ref,
    req_ref,
    kv_hbm,
    bt_ref,
    len_ref,
    dq_hbm,
    dkv_hbm,
    wout_hbm,
    out_ref,
    xv,
    wv,
    kv,
    dq,
    dkv,
    wout,
    acc,
    sq,
    qf,
    qb,
    ac,
    lc,
    vtag,
    rtag,
    tvec,
    tsm,
    slot_of,
    page_of,
    qs,
    qr,
    pacc,
    accs,
    racc,
    sst,
    rst,
    lt,
    sb,
    aall,
    ps,
    pr,
    x_sem,
    in_sem,
    t_sem,
    w_ss,
    w_rs,
    wf_ss,
    tag_ss,
    tag_rs,
    q_ss,
    q_rs,
    a_ss,
    a_rs,
    l_ss,
    l_rs,
    g_ss,
    g_rs,
    gf_ss,
    p_ss,
    p_rs,
):
    me = lax.axis_index("role")
    tp = lax.axis_index("tp")
    chip, core = me // 2, me % 2
    z, yh = chip // 2, chip % 2
    sib = 2 * chip + (1 - core)

    def to_chip(d, sign):
        dz, dy = d // 2, d % 2
        return ((z + sign * dz + 4) % 4) * 2 + (yh + dy) % 2

    def rc(src, dst, ss, rs, role, t=None):
        return pltpu.make_async_remote_copy(
            src_ref=src,
            dst_ref=dst,
            send_sem=ss,
            recv_sem=rs,
            device_id=(role, tp if t is None else t),
            device_id_type=MESH,
        )

    def x_copy(c):
        return pltpu.make_async_copy(x_hbm.at[:, pl.ds(pl.multiple_of(c * KB, KB), KB)], xv.at[c], x_sem.at[c])

    own_w = pltpu.make_async_copy(w_hbm, wv.at[me], in_sem.at[0])
    kv_c = pltpu.make_async_copy(kv_hbm, kv, in_sem.at[1])
    dq_c = pltpu.make_async_copy(dq_hbm, dq, in_sem.at[2])
    dkv_c = pltpu.make_async_copy(dkv_hbm, dkv, in_sem.at[3])
    wout_c = pltpu.make_async_copy(wout_hbm, wout, in_sem.at[4])
    own_w.start()
    dq_c.start()
    dkv_c.start()
    kv_c.start()

    barrier = pltpu.get_barrier_semaphore()

    def greet_role(d, _):
        pl.semaphore_signal(barrier, inc=1, device_id=((me + d) % NR, tp), device_id_type=MESH)
        return 0

    def greet_tp(d, _):
        pl.semaphore_signal(barrier, inc=1, device_id=(me, (tp + d) % NT), device_id_type=MESH)
        return 0

    lax.fori_loop(1, NR, greet_role, 0)
    lax.fori_loop(1, NT, greet_tp, 0)

    lane = lax.broadcasted_iota(jnp.int32, (8, 128), 1)
    owners = [owner_ref[i] for i in range(NP)]
    tags = jnp.full((8, 128), -1, jnp.int32)
    slots = []
    for i in range(NP):
        rank = jnp.int32(0)
        for j in range(i):
            rank = rank + (owners[j] == owners[i]).astype(jnp.int32)
        slot = 2 * owners[i] + rank
        slots.append(slot)
        slot_of[i] = slot
        tags = jnp.where(lane == slot, req_ref[i], tags)
    vtag[...] = tags
    rtag[me] = tags

    own_w.wait()
    pl.semaphore_wait(barrier, NR - 1 + NT - 1)

    def send_tag(d, _):
        p = (me + d) % NR
        rc(vtag, rtag.at[me], tag_ss.at[d], tag_rs.at[me], p).start()
        return 0

    lax.fori_loop(1, NR, send_tag, 0)

    def w_send(d):
        return rc(wv.at[me], wv.at[me], w_ss.at[d], w_rs.at[me], 2 * to_chip(d, 1) + core)

    w_sib = rc(wv.at[me], wv.at[me], w_ss.at[0], w_rs.at[me], sib)
    w_sib.start()

    def start_w(d, _):
        w_send(d).start()
        return 0

    lax.fori_loop(1, 8, start_w, 0)

    x_copy(me).start()
    x_copy(sib).start()

    def start_x(d, _):
        c = to_chip(d, -1)
        x_copy(2 * c + core).start()
        x_copy(2 * c + (1 - core)).start()
        return 0

    lax.fori_loop(1, 8, start_x, 0)
    wout_c.start()

    dq_c.wait()
    for s in range(STEPS):
        for h in range(PER):
            qf[pl.ds(s * PER + h, RQ, stride=RQ), :] = dq[s, :, h * HS : (h + 1) * HS].astype(F32)

    def find_page(s, _):
        i = jnp.int32(0)
        for j in range(NP):
            i = jnp.where(slots[j] == s, j, i)
        page_of[s] = i
        return 0

    lax.fori_loop(0, 2 * NR, find_page, 0)

    acc[...] = jnp.zeros_like(acc)
    sq[...] = jnp.zeros_like(sq)

    dkv_c.wait()
    kv_c.wait()

    def attend(r, _):
        q = qf[pl.ds(pl.multiple_of(r * RQ, RQ), RQ), :].astype(BF)
        qb[r] = q
        pages = [kv[bt_ref[r * 4 + j]] for j in range(4)]
        own = dkv[...]
        keys = jnp.concatenate([p[:, :HS] for p in pages], axis=0)
        values = jnp.concatenate([p[:, HS:] for p in pages], axis=0)
        s1 = lax.dot_general(q, keys, NT_DIMS, preferred_element_type=F32) * SCALING
        s2 = lax.dot_general(q, own[:, :HS], NT_DIMS, preferred_element_type=F32) * SCALING
        col = lax.broadcasted_iota(jnp.int32, s1.shape, 1)
        s1 = jnp.where(col < len_ref[r], s1, LOW)
        col2 = lax.broadcasted_iota(jnp.int32, s2.shape, 1)
        row2 = lax.broadcasted_iota(jnp.int32, s2.shape, 0)
        s2 = jnp.where((col2 % RQ == r) & (col2 // RQ <= row2 // PER), s2, LOW)
        top = jnp.maximum(jnp.max(s1, axis=1, keepdims=True), jnp.max(s2, axis=1, keepdims=True))
        p1 = jnp.exp(s1 - top)
        p2 = jnp.exp(s2 - top)
        total = jnp.sum(p1, axis=1, keepdims=True) + jnp.sum(p2, axis=1, keepdims=True)
        o = jnp.dot(p1.astype(BF), values, preferred_element_type=F32)
        o = o + jnp.dot(p2.astype(BF), own[:, HS:], preferred_element_type=F32)
        ac[pl.ds(r, RQ, stride=RQ), :] = o / total
        lc[pl.ds(r, RQ, stride=RQ), :] = jnp.broadcast_to(top + jnp.log(total), (RQ, HS))
        return 0

    lax.fori_loop(0, RQ, attend, 0)

    tmat = jnp.full((8, 128), -1, jnp.int32)

    def wait_tag(d, t):
        p = (me - d + NR) % NR

        @pl.when(d > 0)
        def _():
            rc(vtag, rtag.at[p], tag_ss.at[0], tag_rs.at[p], p).wait_recv()

        moved = pltpu.roll(rtag[p], (2 * p - 2 * me + 128) % 128, 1)
        return jnp.where(lane // 2 == p, moved, t)

    tmat = lax.fori_loop(0, NR, wait_tag, tmat)
    tvec[...] = tmat
    t_c = pltpu.make_async_copy(tvec, tsm, t_sem)
    t_c.start()
    t_c.wait()

    def pick(s, _):
        qs[s] = qb[jnp.maximum(tsm[0, s], 0)]
        return 0

    lax.fori_loop(0, 2 * NR, pick, 0)

    def send_q(d, _):
        p = (me + d) % NR
        rc(qs.at[pl.ds(2 * p, 2)], qr.at[pl.ds(2 * me, 2)], q_ss.at[d], q_rs.at[me], p).start()
        return 0

    lax.fori_loop(1, NR, send_q, 0)
    qr[pl.ds(2 * me, 2)] = qs[pl.ds(2 * me, 2)]

    def project(c):
        x_copy(c).wait()

        def tile(t, _):
            rows = pl.ds(pl.multiple_of(t * TILE, TILE), TILE)
            xa = xv[c, rows, :]
            acc[rows, :] += jnp.dot(xa, wv[c], preferred_element_type=F32)
            xf = xa.astype(F32)
            xx = xf * xf
            sq[rows, :] += (xx[:, :128] + xx[:, 128:256]) + (xx[:, 256:384] + xx[:, 384:])
            return 0

        lax.fori_loop(0, ROWS // TILE, tile, 0)

    def w_recv(p):
        rc(wv.at[p], wv.at[p], w_ss.at[0], w_rs.at[p], sib).wait_recv()

    def w_fwd(d, p):
        return rc(wv.at[p], wv.at[p], wf_ss.at[d], w_rs.at[p], sib)

    project(me)
    w_recv(sib)
    project(sib)

    def arrive(d, _):
        c = to_chip(d, -1)
        w_recv(2 * c + core)
        w_fwd(d, 2 * c + core).start()
        project(2 * c + core)
        w_recv(2 * c + (1 - core))
        project(2 * c + (1 - core))
        return 0

    lax.fori_loop(1, 8, arrive, 0)

    def wait_q(d, _):
        p = (me - d + NR) % NR
        rc(qs.at[pl.ds(0, 2)], qr.at[pl.ds(2 * p, 2)], q_ss.at[0], q_rs.at[p], p).wait_recv()
        return 0

    lax.fori_loop(1, NR, wait_q, 0)
    bias = bias_ref[...].astype(F32)
    lane_k = lax.broadcasted_iota(jnp.int32, (RQ, 128), 1)

    def page(i, st):
        rows = pl.ds(pl.multiple_of(i * PAGE, PAGE), PAGE)
        inverse = lax.rsqrt(jnp.sum(sq[rows, :], axis=1, keepdims=True) * (1.0 / (NR * KB)) + EPSILON)
        f = (acc[rows, :] * inverse + bias).astype(BF)
        slot = slot_of[i]
        q = qr[slot]
        s = lax.dot_general(q, f[:, :HS], NT_DIMS, preferred_element_type=F32) * SCALING
        top = jnp.max(s, axis=1, keepdims=True)
        p = jnp.exp(s - top)
        total = jnp.sum(p, axis=1, keepdims=True)
        o = jnp.dot(p.astype(BF), f[:, HS:], preferred_element_type=F32) / total
        pacc[i] = o.astype(BF)
        return jnp.where(lane_k == slot, top + jnp.log(total), st)

    st = lax.fori_loop(0, NP, page, jnp.full((RQ, 128), LOW, F32))
    packed = st[0:8]
    for a in range(1, 4):
        packed = jnp.where(lane // 32 == a, pltpu.roll(st[8 * a : 8 * a + 8], 32 * a, 1), packed)
    sst[...] = packed
    rst[me] = packed

    def place(s, _):
        accs[s] = pacc[page_of[s]]
        return 0

    lax.fori_loop(0, 2 * NR, place, 0)

    def send_acc(d, _):
        p = (me + d) % NR
        rc(accs.at[pl.ds(2 * p, 2)], racc.at[pl.ds(2 * me, 2)], a_ss.at[d], a_rs.at[me], p).start()
        rc(sst, rst.at[me], l_ss.at[d], l_rs.at[me], p).start()
        return 0

    lax.fori_loop(1, NR, send_acc, 0)
    racc[pl.ds(2 * me, 2)] = accs[pl.ds(2 * me, 2)]

    lt[...] = jnp.full((RQ, 128), LOW, F32)

    def take(d, _):
        p = (me - d + NR) % NR

        @pl.when(d > 0)
        def _():
            rc(sst, rst.at[p], l_ss.at[0], l_rs.at[p], p).wait_recv()
            rc(accs.at[pl.ds(0, 2)], racc.at[pl.ds(2 * p, 2)], a_ss.at[0], a_rs.at[p], p).wait_recv()

        got = rst[p]
        for a in range(4):
            moved = pltpu.roll(got, (2 * p - 2 * me - 32 * a + 256) % 128, 1)
            lt[8 * a : 8 * a + 8, :] = jnp.where(lane // 2 == p, moved, lt[8 * a : 8 * a + 8, :])
        for c in range(2):
            sb[pl.ds(2 * p + c, RQ, stride=RQ), :] = racc[2 * p + c].astype(F32)
        return 0

    lax.fori_loop(0, NR, take, 0)

    mine = jnp.broadcast_to(tvec[0:1, :], (RQ, 128)) == lax.broadcasted_iota(jnp.int32, (RQ, 128), 0)

    def g_send(s, d):
        role = jnp.where(d == 0, sib, 2 * to_chip(d, 1) + core)
        return rc(aall.at[s, me], aall.at[s, me], g_ss.at[s, d], g_rs.at[s, me], role)

    def merge(s, _):
        for h in range(PER):
            k = s * PER + h
            rows = pl.ds(pl.multiple_of(k * RQ, RQ), RQ)
            scores = jnp.where(mine, jnp.broadcast_to(lt[pl.ds(k, 1), :], (RQ, 128)), LOW)
            base = lc[rows, :]
            top = jnp.maximum(jnp.max(scores, axis=1, keepdims=True), base)
            e = jnp.exp(scores - top)
            wc = jnp.exp(base - top)
            total = wc + jnp.sum(e, axis=1, keepdims=True)
            pv = jnp.dot(e[:, : 2 * NR].astype(BF), sb[rows, :].astype(BF), preferred_element_type=F32)
            merged = (wc * ac[rows, :] + pv) / total
            aall[s, me, :, h * HS : (h + 1) * HS] = merged.astype(BF)

        def start_g(d, _):
            g_send(s, d).start()
            return 0

        lax.fori_loop(0, 8, start_g, 0)
        return 0

    lax.fori_loop(0, STEPS, merge, 0)
    wout_c.wait()

    def g_recv(s, p):
        rc(aall.at[s, p], aall.at[s, p], g_ss.at[s, 0], g_rs.at[s, p], sib).wait_recv()

    def g_fwd(s, d, p):
        return rc(aall.at[s, p], aall.at[s, p], gf_ss.at[s, d], g_rs.at[s, p], sib)

    def p_send(s, d):
        t = (tp + d) % NT
        return rc(ps.at[s, t], pr.at[tp, s], p_ss.at[s, d], p_rs.at[s, tp], me, t)

    def finish(s, _):
        def pass_on(d, _):
            p = 2 * to_chip(d, -1) + core
            g_recv(s, p)
            g_fwd(s, d, p).start()
            return 0

        lax.fori_loop(1, 8, pass_on, 0)
        g_recv(s, sib)

        def other(d, _):
            g_recv(s, 2 * to_chip(d, -1) + (1 - core))
            return 0

        lax.fori_loop(1, 8, other, 0)

        def part(j, _):
            a = aall[s, pl.ds(j * 8, 8)].reshape(8 * RQ, 1024)
            o = jnp.dot(a, wout[...], preferred_element_type=F32).astype(BF)
            ps[s, pl.ds(j * 4, 4)] = o.reshape(4, 2 * RQ, NOUT)
            return 0

        lax.fori_loop(0, 2, part, 0)

        def start_p(d, _):
            p_send(s, d).start()
            return 0

        lax.fori_loop(1, NT, start_p, 0)
        return 0

    lax.fori_loop(0, STEPS, finish, 0)

    def total_of(s, _):
        def add(d, o):
            t = (tp - d + NT) % NT
            rc(ps.at[s, 0], pr.at[t, s], p_ss.at[s, 0], p_rs.at[s, t], me, t).wait_recv()
            return o

        lax.fori_loop(1, NT, add, 0)
        o = ps[s, tp].astype(F32)
        for d in range(1, NT):
            o = o + pr[(tp + d) % NT, s].astype(F32)
        out_ref[s] = o.astype(BF)
        return 0

    lax.fori_loop(0, STEPS, total_of, 0)

    def drain(d, _):
        rc(vtag, rtag.at[me], tag_ss.at[d], tag_rs.at[me], sib).wait_send()
        rc(qs.at[pl.ds(0, 2)], qr.at[pl.ds(0, 2)], q_ss.at[d], q_rs.at[me], sib).wait_send()
        rc(accs.at[pl.ds(0, 2)], racc.at[pl.ds(0, 2)], a_ss.at[d], a_rs.at[me], sib).wait_send()
        rc(sst, rst.at[me], l_ss.at[d], l_rs.at[me], sib).wait_send()
        return 0

    lax.fori_loop(1, NR, drain, 0)
    w_sib.wait_send()

    def drain_w(d, _):
        w_send(d).wait_send()
        w_fwd(d, me).wait_send()
        return 0

    lax.fori_loop(1, 8, drain_w, 0)

    def drain_g(s, _):
        def one(d, _):
            g_send(s, d).wait_send()

            @pl.when(d > 0)
            def _():
                g_fwd(s, d, me).wait_send()
                p_send(s, d).wait_send()

            return 0

        lax.fori_loop(0, 8, one, 0)
        return 0

    lax.fori_loop(0, STEPS, drain_g, 0)


def body(
    x_pre,
    ln_gain,
    w_kv,
    kv_bias,
    page_owner,
    page_req,
    kv_pool,
    block_table,
    cache_len,
    dec_q,
    dec_kv,
    w_out,
):
    gain = lax.dynamic_slice_in_dim(ln_gain, lax.axis_index("role") * KB, KB, 0)
    scaled = (w_kv.astype(F32) * gain.astype(F32)[:, None]).astype(BF)
    any_spec = pl.BlockSpec(memory_space=pl.ANY)
    smem = pl.BlockSpec(memory_space=pltpu.SMEM)
    vmem = pl.BlockSpec(memory_space=pltpu.VMEM)
    dma = pltpu.SemaphoreType.DMA
    V = pltpu.VMEM
    scratch = [
        V((NR, ROWS, KB), BF),
        V((NR, KB, KVW), BF),
        V((32, PAGE, KVW), BF),
        V((STEPS, RQ, 1024), BF),
        V((STEPS * RQ, KVW), BF),
        V((1024, NOUT), BF),
        V((ROWS, KVW), F32),
        V((ROWS, 128), F32),
        V((RQ * RQ, HS), F32),
        V((RQ, RQ, HS), BF),
        V((RQ * RQ, HS), F32),
        V((RQ * RQ, HS), F32),
        V((8, 128), jnp.int32),
        V((NR, 8, 128), jnp.int32),
        V((8, 128), jnp.int32),
        pltpu.SMEM((8, 128), jnp.int32),
        pltpu.SMEM((16,), jnp.int32),
        pltpu.SMEM((2 * NR,), jnp.int32),
        V((2 * NR, RQ, HS), BF),
        V((2 * NR, RQ, HS), BF),
        V((NP, RQ, HS), BF),
        V((2 * NR, RQ, HS), BF),
        V((2 * NR, RQ, HS), BF),
        V((8, 128), F32),
        V((NR, 8, 128), F32),
        V((RQ, 128), F32),
        V((RQ * RQ, HS), F32),
        V((STEPS, NR, RQ, 1024), BF),
        V((STEPS, NT, 2 * RQ, NOUT), BF),
        V((NT, STEPS, 2 * RQ, NOUT), BF),
        dma((NR,)),
        dma((5,)),
        dma,
        dma((8,)),
        dma((NR,)),
        dma((8,)),
        dma((NR,)),
        dma((NR,)),
        dma((NR,)),
        dma((NR,)),
        dma((NR,)),
        dma((NR,)),
        dma((NR,)),
        dma((NR,)),
        dma((STEPS, 8)),
        dma((STEPS, NR)),
        dma((STEPS, 8)),
        dma((STEPS, 8)),
        dma((STEPS, NT)),
    ]
    return pl.pallas_call(
        kernel,
        out_shape=jax.ShapeDtypeStruct((STEPS, 2 * RQ, NOUT), BF),
        in_specs=[any_spec, any_spec, vmem, smem, smem, any_spec, smem, smem, any_spec, any_spec, any_spec],
        out_specs=vmem,
        scratch_shapes=scratch,
        compiler_params=pltpu.CompilerParams(
            collective_id=0, has_side_effects=True, vmem_limit_bytes=58 * 1024 * 1024
        ),
    )(
        x_pre,
        scaled,
        kv_bias.reshape(1, KVW),
        page_owner.reshape(NP),
        page_req,
        kv_pool,
        block_table.reshape(RQ * 4),
        cache_len,
        dec_q,
        dec_kv.reshape(STEPS * RQ, KVW),
        w_out,
    )


def solution(mesh):
    return jax.shard_map(
        body,
        mesh=mesh,
        in_specs=(
            P("role", None),
            P(),
            P("role", "tp"),
            P("tp"),
            P("role", None),
            P("role"),
            P("role", None, "tp"),
            P("role", None),
            P("role"),
            P(None, "role", "tp"),
            P(None, "role", "tp"),
            P("tp", "role"),
        ),
        out_specs=P(None, "tp", "role"),
        check_vma=False,
    )
```

```python
import functools
import math

import jax
import jax.numpy as jnp
from jax import lax
from jax.experimental import pallas as pl
from jax.experimental.pallas import tpu as pltpu
from jax.sharding import PartitionSpec as P

HS = 128
PAGE = 128
EPSILON = 1e-06
LOW = -1e30
MESH = pl.DeviceIdType.MESH
BF = jnp.bfloat16
F32 = jnp.float32

NR = 16
NT = 8
NP = 11
RQ = 32
STEPS = 4
PER = 8
KB = 512
KVW = 256
ROWS = NP * PAGE
TILE = 352
UNROLL = 2
NOUT = 512
SCALING = 1.0 / math.sqrt(HS)
NT_DIMS = (((1,), (1,)), ((), ()))


def kernel(
    x_hbm,
    gain_ref,
    w_hbm,
    bias_ref,
    owner_ref,
    req_ref,
    kv_hbm,
    bt_ref,
    len_ref,
    dq_hbm,
    dkv_hbm,
    wout_hbm,
    out_ref,
    xv,
    wraw,
    wv,
    kv,
    dq,
    dkv,
    wout,
    acc,
    sq,
    qf,
    qb,
    ac,
    lc,
    vtag,
    rtag,
    tvec,
    tsm,
    slot_of,
    page_of,
    qs,
    qr,
    pacc,
    accs,
    racc,
    sst,
    rst,
    lt,
    sb,
    aall,
    ps,
    px,
    ys,
    py,
    ko,
    x_sem,
    in_sem,
    t_sem,
    w_ss,
    w_rs,
    tag_ss,
    tag_rs,
    q_ss,
    q_rs,
    a_ss,
    a_rs,
    l_ss,
    l_rs,
    g_ss,
    g_rs,
    p_ss,
    p_rs,
    y_ss,
    y_rs,
):
    me = lax.axis_index("role")
    tp = lax.axis_index("tp")
    chip, core = me // 2, me % 2
    z, yh = chip // 2, chip % 2
    yl, xx = tp // 4, tp % 4
    sib = 2 * chip + (1 - core)

    def chip_at(dz, dy):
        return ((z + dz) % 4) * 2 + (yh + dy) % 2

    c_y, c_p, c_m, c_2 = chip_at(0, 1), chip_at(1, 0), chip_at(3, 0), chip_at(2, 0)
    c_yp, c_ym, c_y2 = chip_at(1, 1), chip_at(3, 1), chip_at(2, 1)

    def rc(src, dst, ss, rs, role, t=None):
        return pltpu.make_async_remote_copy(
            src_ref=src,
            dst_ref=dst,
            send_sem=ss,
            recv_sem=rs,
            device_id=(role, tp if t is None else t),
            device_id_type=MESH,
        )

    class Gather:
        def __init__(self, block, ss, rs):
            self.block, self.ss, self.rs = block, ss, rs

        def copy(self, i, of, to):
            return rc(self.block(of), self.block(of), self.ss(i), self.rs(of), to)

        def ops(self):
            ch = lambda c: 2 * c + core
            return [
                (me, ch(c_y)),
                (me, ch(c_p)),
                (me, ch(c_m)),
                (me, ch(c_2)),
                (me, sib),
                (ch(c_y), ch(c_p)),
                (ch(c_y), ch(c_m)),
                (ch(c_2), ch(c_y)),
            ] + [(ch(c), sib) for c in (c_p, c_m, c_y, c_2, c_yp, c_ym, c_y2)]

        def start(self, *which):
            ops = self.ops()
            for i in which:
                self.copy(i, *ops[i]).start()

        def wait(self, role):
            self.copy(0, role, sib).wait_recv()

        def first(self):
            self.start(0, 1, 2, 3, 4)

        def relay(self):
            self.wait(2 * c_y + core)
            self.start(5, 6, 10)
            self.wait(2 * c_2 + core)
            self.start(7, 11)
            self.wait(2 * c_p + core)
            self.start(8)
            self.wait(2 * c_m + core)
            self.start(9)

        def late(self):
            for i, c in ((12, c_yp), (13, c_ym), (14, c_y2)):
                self.wait(2 * c + core)
                self.start(i)

        def from_sib(self, c):
            self.wait(2 * c + (1 - core))

        def drain(self):
            ops = self.ops()
            for i in range(15):
                self.copy(i, *ops[i]).wait_send()

    def x_copy(c):
        return pltpu.make_async_copy(
            x_hbm.at[:, pl.ds(pl.multiple_of(c * 2 * KB, 2 * KB), 2 * KB)], xv.at[c], x_sem.at[c]
        )

    w_c = pltpu.make_async_copy(w_hbm, wraw, in_sem.at[0])
    kv_c = pltpu.make_async_copy(kv_hbm, kv, in_sem.at[1])
    dq_c = pltpu.make_async_copy(dq_hbm, dq, in_sem.at[2])
    dkv_c = pltpu.make_async_copy(dkv_hbm, dkv, in_sem.at[3])
    wout_c = pltpu.make_async_copy(wout_hbm, wout, in_sem.at[4])
    w_c.start()
    dq_c.start()
    dkv_c.start()
    kv_c.start()

    barrier = pltpu.get_barrier_semaphore()

    def greet_role(d, _):
        pl.semaphore_signal(barrier, inc=1, device_id=((me + d) % NR, tp), device_id_type=MESH)
        return 0

    lax.fori_loop(1, NR, greet_role, 0)
    for d in range(1, 4):
        pl.semaphore_signal(barrier, inc=1, device_id=(me, 4 * yl + (xx + d) % 4), device_id_type=MESH)
    pl.semaphore_signal(barrier, inc=1, device_id=(me, 4 * (1 - yl) + xx), device_id_type=MESH)

    chips = (chip, c_p, c_m, c_y, c_2, c_yp, c_ym, c_y2)
    for c in chips:
        x_copy(c).start()
    wout_c.start()

    lane = lax.broadcasted_iota(jnp.int32, (8, 128), 1)
    owners = [owner_ref[i, 0] for i in range(NP)]
    tags = jnp.full((8, 128), -1, jnp.int32)
    slots = []
    for i in range(NP):
        rank = jnp.int32(0)
        for j in range(i):
            rank = rank + (owners[j] == owners[i]).astype(jnp.int32)
        slot = 2 * owners[i] + rank
        slots.append(slot)
        slot_of[i] = slot
        tags = jnp.where(lane == slot, req_ref[i], tags)
    vtag[...] = tags
    rtag[me] = tags

    w_c.wait()
    eye = lax.broadcasted_iota(jnp.int32, (128, 128), 0) == lax.broadcasted_iota(jnp.int32, (128, 128), 1)
    for i in range(KB // 128):
        g = jnp.broadcast_to(gain_ref[me, i : i + 1, :], (128, 128))
        g = jnp.sum(jnp.where(eye, g, 0.0), axis=1, keepdims=True)
        rows = slice(128 * i, 128 * i + 128)
        wv[me, rows, :] = (wraw[rows, :].astype(F32) * g).astype(BF)

    dq_c.wait()
    for s in range(STEPS):
        for h in range(PER):
            qf[pl.ds(s * PER + h, RQ, stride=RQ), :] = dq[s, :, h * HS : (h + 1) * HS].astype(F32)

    def by_request(r, _):
        qb[r] = qf[pl.ds(pl.multiple_of(r * RQ, RQ), RQ), :].astype(BF)
        return 0

    lax.fori_loop(0, RQ, by_request, 0, unroll=4)

    pl.semaphore_wait(barrier, NR - 1 + 4)

    def send_tag(d, _):
        p = (me + d) % NR
        rc(vtag, rtag.at[me], tag_ss.at[d], tag_rs.at[me], p).start()
        return 0

    lax.fori_loop(1, NR, send_tag, 0)
    w_all = Gather(lambda r: wv.at[r], lambda i: w_ss.at[i], lambda r: w_rs.at[r])
    w_all.first()

    def find_page(s, _):
        i = jnp.int32(0)
        for j in range(NP):
            i = jnp.where(slots[j] == s, j, i)
        page_of[s] = i
        return 0

    lax.fori_loop(0, 2 * NR, find_page, 0)

    acc[...] = jnp.zeros_like(acc)
    sq[...] = jnp.zeros_like(sq)

    dkv_c.wait()
    kv_c.wait()

    def attend(r, _):
        q = qb[r]
        pages = [kv[bt_ref[r, j]] for j in range(4)]
        own = dkv[...]
        keys = jnp.concatenate([p[:, :HS] for p in pages], axis=0)
        values = jnp.concatenate([p[:, HS:] for p in pages], axis=0)
        s1 = lax.dot_general(q, keys, NT_DIMS, preferred_element_type=F32) * SCALING
        s2 = lax.dot_general(q, own[:, :HS], NT_DIMS, preferred_element_type=F32) * SCALING
        col = lax.broadcasted_iota(jnp.int32, s1.shape, 1)
        s1 = jnp.where(col < len_ref[r], s1, LOW)
        col2 = lax.broadcasted_iota(jnp.int32, s2.shape, 1)
        row2 = lax.broadcasted_iota(jnp.int32, s2.shape, 0)
        s2 = jnp.where((col2 % RQ == r) & (col2 // RQ <= row2 // PER), s2, LOW)
        top = jnp.maximum(jnp.max(s1, axis=1, keepdims=True), jnp.max(s2, axis=1, keepdims=True))
        p1 = jnp.exp(s1 - top)
        p2 = jnp.exp(s2 - top)
        total = jnp.sum(p1, axis=1, keepdims=True) + jnp.sum(p2, axis=1, keepdims=True)
        o = jnp.dot(p1.astype(BF), values, preferred_element_type=F32)
        o = o + jnp.dot(p2.astype(BF), own[:, HS:], preferred_element_type=F32)
        ac[pl.ds(r, RQ, stride=RQ), :] = o / total
        lc[pl.ds(r, RQ, stride=RQ), :] = jnp.broadcast_to(top + jnp.log(total), (RQ, HS))
        return 0

    lax.fori_loop(0, RQ // 2, attend, 0, unroll=UNROLL)

    tmat = jnp.full((8, 128), -1, jnp.int32)

    def wait_tag(d, t):
        p = (me - d + NR) % NR

        @pl.when(d > 0)
        def _():
            rc(vtag, rtag.at[p], tag_ss.at[0], tag_rs.at[p], p).wait_recv()

        moved = pltpu.roll(rtag[p], (2 * p - 2 * me + 128) % 128, 1)
        return jnp.where(lane // 2 == p, moved, t)

    tmat = lax.fori_loop(0, NR, wait_tag, tmat)
    tvec[...] = tmat
    t_c = pltpu.make_async_copy(tvec, tsm, t_sem)
    t_c.start()
    t_c.wait()

    def pick(s, _):
        qs[s] = qb[jnp.maximum(tsm[0, s], 0)]
        return 0

    lax.fori_loop(0, 2 * NR, pick, 0, unroll=4)

    def send_q(d, _):
        p = (me + d) % NR
        rc(qs.at[pl.ds(2 * p, 2)], qr.at[pl.ds(2 * me, 2)], q_ss.at[d], q_rs.at[me], p).start()
        return 0

    lax.fori_loop(1, NR, send_q, 0)
    qr[pl.ds(2 * me, 2)] = qs[pl.ds(2 * me, 2)]

    w_all.relay()
    lax.fori_loop(RQ // 2, RQ, attend, 0, unroll=UNROLL)

    def project(c):
        x_copy(c).wait()

        def tile(t, _):
            rows = pl.ds(pl.multiple_of(t * TILE, TILE), TILE)
            xa = xv[c, rows, :]
            acc[rows, :] += jnp.dot(xa, wv[pl.ds(2 * c, 2)].reshape(2 * KB, KVW), preferred_element_type=F32)
            part = sq[rows, :]
            for i in range(2 * KB // 128):
                xf = xa[:, i * 128 : i * 128 + 128].astype(F32)
                part = part + xf * xf
            sq[rows, :] = part
            return 0

        lax.fori_loop(0, ROWS // TILE, tile, 0)

    w_all.wait(sib)
    project(chip)
    for c in (c_p, c_m, c_y, c_2):
        w_all.from_sib(c)
        project(c)
    w_all.late()
    for c in (c_yp, c_ym, c_y2):
        w_all.from_sib(c)
        project(c)

    def wait_q(d, _):
        p = (me - d + NR) % NR
        rc(qs.at[pl.ds(0, 2)], qr.at[pl.ds(2 * p, 2)], q_ss.at[0], q_rs.at[p], p).wait_recv()
        return 0

    lax.fori_loop(1, NR, wait_q, 0)
    bias = bias_ref[...].astype(F32)
    lane_k = lax.broadcasted_iota(jnp.int32, (RQ, 128), 1)

    def page(i, st):
        rows = pl.ds(pl.multiple_of(i * PAGE, PAGE), PAGE)
        inverse = lax.rsqrt(jnp.sum(sq[rows, :], axis=1, keepdims=True) * (1.0 / (NR * KB)) + EPSILON)
        f = (acc[rows, :] * inverse + bias).astype(BF)
        slot = slot_of[i]
        q = qr[slot]
        s = lax.dot_general(q, f[:, :HS], NT_DIMS, preferred_element_type=F32) * SCALING
        top = jnp.max(s, axis=1, keepdims=True)
        p = jnp.exp(s - top)
        total = jnp.sum(p, axis=1, keepdims=True)
        o = jnp.dot(p.astype(BF), f[:, HS:], preferred_element_type=F32) / total
        pacc[i] = o.astype(BF)
        return jnp.where(lane_k == slot, top + jnp.log(total), st)

    st = lax.fori_loop(0, NP, page, jnp.full((RQ, 128), LOW, F32), unroll=True)
    packed = st[0:8]
    for a in range(1, 4):
        packed = jnp.where(lane // 32 == a, pltpu.roll(st[8 * a : 8 * a + 8], 32 * a, 1), packed)
    sst[...] = packed
    rst[me] = packed

    def place(s, _):
        accs[s] = pacc[page_of[s]]
        return 0

    lax.fori_loop(0, 2 * NR, place, 0, unroll=4)

    def send_acc(d, _):
        p = (me + d) % NR
        rc(accs.at[pl.ds(2 * p, 2)], racc.at[pl.ds(2 * me, 2)], a_ss.at[d], a_rs.at[me], p).start()
        rc(sst, rst.at[me], l_ss.at[d], l_rs.at[me], p).start()
        return 0

    lax.fori_loop(1, NR, send_acc, 0)
    racc[pl.ds(2 * me, 2)] = accs[pl.ds(2 * me, 2)]

    lt[...] = jnp.full((RQ, 128), LOW, F32)

    def wait_acc(d, _):
        p = (me - d + NR) % NR
        rc(sst, rst.at[p], l_ss.at[0], l_rs.at[p], p).wait_recv()
        rc(accs.at[pl.ds(0, 2)], racc.at[pl.ds(2 * p, 2)], a_ss.at[0], a_rs.at[p], p).wait_recv()
        return 0

    lax.fori_loop(1, NR, wait_acc, 0)

    def take(p, _):
        got = rst[p]
        for a in range(4):
            moved = pltpu.roll(got, (2 * p - 2 * me - 32 * a + 256) % 128, 1)
            lt[8 * a : 8 * a + 8, :] = jnp.where(lane // 2 == p, moved, lt[8 * a : 8 * a + 8, :])
        for c in range(2):
            sb[pl.ds(2 * p + c, RQ, stride=RQ), :] = racc[2 * p + c].astype(F32)
        return 0

    lax.fori_loop(0, NR, take, 0, unroll=4)

    mine = jnp.broadcast_to(tvec[0:1, :], (RQ, 128)) == lax.broadcasted_iota(jnp.int32, (RQ, 128), 0)

    def outputs(s):
        return Gather(lambda r: aall.at[s, r], lambda i: g_ss.at[s, i], lambda r: g_rs.at[s, r])

    def merge(s):
        for h in range(PER):
            k = s * PER + h
            rows = pl.ds(pl.multiple_of(k * RQ, RQ), RQ)
            scores = jnp.where(mine, jnp.broadcast_to(lt[pl.ds(k, 1), :], (RQ, 128)), LOW)
            base = lc[rows, :]
            top = jnp.maximum(jnp.max(scores, axis=1, keepdims=True), base)
            e = jnp.exp(scores - top)
            wc = jnp.exp(base - top)
            total = wc + jnp.sum(e, axis=1, keepdims=True)
            pv = jnp.dot(e[:, : 2 * NR].astype(BF), sb[rows, :].astype(BF), preferred_element_type=F32)
            merged = (wc * ac[rows, :] + pv) / total
            aall[s, me, :, h * HS : (h + 1) * HS] = merged.astype(BF)
        outputs(s).first()

    def x_send(s, d):
        to = (xx + d) % 4
        return rc(ps.at[s, to], px.at[s, xx], p_ss.at[s, d], p_rs.at[s, xx], me, 4 * yl + to)

    def x_wait(s, d):
        of = (xx + d) % 4
        rc(ps.at[s, 0], px.at[s, of], p_ss.at[s, 0], p_rs.at[s, of], me, 4 * yl + of).wait_recv()

    def y_send(s):
        return rc(ys.at[s], py.at[s], y_ss.at[s], y_rs.at[s], me, 4 * (1 - yl) + xx)

    def product(s):
        g = outputs(s)
        g.late()
        g.wait(sib)
        for c in chips[1:]:
            g.from_sib(c)

        def part(j, _):
            a = aall[s, pl.ds(j * 8, 8)].reshape(8 * RQ, 1024)
            o = jnp.dot(a, wout[...], preferred_element_type=F32).astype(BF)
            o = o.reshape(4, 2 * RQ, NOUT)
            for i in range(4):
                ps[s, i, j] = o[i]
            return 0

        lax.fori_loop(0, 2, part, 0)
        for d in range(1, 4):
            x_send(s, d).start()

    def add_x(s):
        for d in range(1, 4):
            x_wait(s, d)
        for half in range(2):
            o = ps[s, xx, half].astype(F32)
            for d in range(1, 4):
                o = o + px[s, (xx + d) % 4, half].astype(F32)

            @pl.when(yl == half)
            def _():
                ko[s] = o

            @pl.when(yl != half)
            def _():
                ys[s] = o.astype(BF)

        y_send(s).start()

    def add_y(s):
        y_send(s).wait_recv()
        out_ref[s] = (ko[s] + py[s].astype(F32)).astype(BF)

    merge(0)
    merge(1)
    wout_c.wait()

    def round_(i, _):
        @pl.when(i < STEPS)
        def _():
            outputs(i).relay()

        @pl.when(i < STEPS - 2)
        def _():
            merge(i + 2)

        @pl.when((i >= 1) & (i <= STEPS))
        def _():
            product(i - 1)

        @pl.when((i >= 2) & (i <= STEPS + 1))
        def _():
            add_x(i - 2)

        @pl.when(i >= 3)
        def _():
            add_y(i - 3)

        return 0

    lax.fori_loop(0, STEPS + 3, round_, 0)

    def drain(d, _):
        rc(vtag, rtag.at[me], tag_ss.at[d], tag_rs.at[me], sib).wait_send()
        rc(qs.at[pl.ds(0, 2)], qr.at[pl.ds(0, 2)], q_ss.at[d], q_rs.at[me], sib).wait_send()
        rc(accs.at[pl.ds(0, 2)], racc.at[pl.ds(0, 2)], a_ss.at[d], a_rs.at[me], sib).wait_send()
        rc(sst, rst.at[me], l_ss.at[d], l_rs.at[me], sib).wait_send()
        return 0

    lax.fori_loop(1, NR, drain, 0)
    w_all.drain()

    def drain_s(s, _):
        outputs(s).drain()
        for d in range(1, 4):
            x_send(s, d).wait_send()
        y_send(s).wait_send()
        return 0

    lax.fori_loop(0, STEPS, drain_s, 0)


def body(
    x_pre,
    ln_gain,
    w_kv,
    kv_bias,
    page_owner,
    page_req,
    kv_pool,
    block_table,
    cache_len,
    dec_q,
    dec_kv,
    w_out,
):
    any_spec = pl.BlockSpec(memory_space=pl.ANY)
    smem = pl.BlockSpec(memory_space=pltpu.SMEM)
    vmem = pl.BlockSpec(memory_space=pltpu.VMEM)
    dma = pltpu.SemaphoreType.DMA
    V = pltpu.VMEM
    scratch = [
        V((8, ROWS, 2 * KB), BF),
        V((KB, KVW), BF),
        V((NR, KB, KVW), BF),
        V((32, PAGE, KVW), BF),
        V((STEPS, RQ, 1024), BF),
        V((STEPS * RQ, KVW), BF),
        V((1024, NOUT), BF),
        V((ROWS, KVW), F32),
        V((ROWS, 128), F32),
        V((RQ * RQ, HS), F32),
        V((RQ, RQ, HS), BF),
        V((RQ * RQ, HS), F32),
        V((RQ * RQ, HS), F32),
        V((8, 128), jnp.int32),
        V((NR, 8, 128), jnp.int32),
        V((8, 128), jnp.int32),
        pltpu.SMEM((8, 128), jnp.int32),
        pltpu.SMEM((16,), jnp.int32),
        pltpu.SMEM((2 * NR,), jnp.int32),
        V((2 * NR, RQ, HS), BF),
        V((2 * NR, RQ, HS), BF),
        V((NP, RQ, HS), BF),
        V((2 * NR, RQ, HS), BF),
        V((2 * NR, RQ, HS), BF),
        V((8, 128), F32),
        V((NR, 8, 128), F32),
        V((RQ, 128), F32),
        V((RQ * RQ, HS), F32),
        V((STEPS, NR, RQ, 1024), BF),
        V((STEPS, 4, 2, 2 * RQ, NOUT), BF),
        V((STEPS, 4, 2, 2 * RQ, NOUT), BF),
        V((STEPS, 2 * RQ, NOUT), BF),
        V((STEPS, 2 * RQ, NOUT), BF),
        V((STEPS, 2 * RQ, NOUT), F32),
        dma((8,)),
        dma((5,)),
        dma,
        dma((15,)),
        dma((NR,)),
        dma((NR,)),
        dma((NR,)),
        dma((NR,)),
        dma((NR,)),
        dma((NR,)),
        dma((NR,)),
        dma((NR,)),
        dma((NR,)),
        dma((STEPS, 15)),
        dma((STEPS, NR)),
        dma((STEPS, 4)),
        dma((STEPS, 4)),
        dma((STEPS,)),
        dma((STEPS,)),
    ]
    return pl.pallas_call(
        kernel,
        out_shape=jax.ShapeDtypeStruct((STEPS, 2 * RQ, NOUT), BF),
        in_specs=[any_spec, vmem, any_spec, vmem, smem, smem, any_spec, smem, smem, any_spec, any_spec, any_spec],
        out_specs=vmem,
        scratch_shapes=scratch,
        compiler_params=pltpu.CompilerParams(
            collective_id=0, has_side_effects=True, vmem_limit_bytes=58 * 1024 * 1024
        ),
    )(
        x_pre,
        ln_gain.reshape(NR, KB // 128, 128).astype(F32),
        w_kv,
        kv_bias.reshape(1, KVW),
        page_owner,
        page_req,
        kv_pool,
        block_table,
        cache_len,
        dec_q,
        dec_kv.reshape(STEPS * RQ, KVW),
        w_out,
    )


def solution(mesh):
    return jax.shard_map(
        body,
        mesh=mesh,
        in_specs=(
            P("role", None),
            P(),
            P("role", "tp"),
            P("tp"),
            P("role", None),
            P("role"),
            P("role", None, "tp"),
            P("role", None),
            P("role"),
            P(None, "role", "tp"),
            P(None, "role", "tp"),
            P("tp", "role"),
        ),
        out_specs=P(None, "tp", "role"),
        check_vma=False,
    )
```

```python
import functools
import math

import jax
import jax.numpy as jnp
from jax import lax
from jax.experimental import pallas as pl
from jax.experimental.pallas import tpu as pltpu
from jax.sharding import PartitionSpec as P

HS = 128
PAGE = 128
EPSILON = 1e-06
LOW = -1e30
MESH = pl.DeviceIdType.MESH
BF = jnp.bfloat16
F32 = jnp.float32

NR = 16
NT = 8
NP = 11
RQ = 32
STEPS = 4
PER = 8
KB = 512
KVW = 256
ROWS = NP * PAGE
TILE = 704
UNROLL = 4
NOUT = 512
SCALING = 1.0 / math.sqrt(HS)
NT_DIMS = (((1,), (1,)), ((), ()))


def kernel(
    x_hbm,
    gain_ref,
    w_hbm,
    bias_ref,
    owner_ref,
    req_ref,
    kv_hbm,
    bt_ref,
    len_ref,
    dq_hbm,
    dkv_hbm,
    wout_hbm,
    out_ref,
    xv,
    wraw,
    wv,
    kv,
    dq,
    dkv,
    wout,
    acc,
    sq,
    qf,
    qb,
    ac,
    lc,
    vtag,
    rtag,
    tvec,
    tsm,
    slot_of,
    page_of,
    qs,
    qr,
    pacc,
    accs,
    racc,
    sst,
    rst,
    lt,
    sb,
    aall,
    ps,
    px,
    ys,
    py,
    ko,
    x_sem,
    in_sem,
    t_sem,
    w_ss,
    w_rs,
    tag_ss,
    tag_rs,
    q_ss,
    q_rs,
    a_ss,
    a_rs,
    l_ss,
    l_rs,
    g_ss,
    g_rs,
    p_ss,
    p_rs,
    y_ss,
    y_rs,
):
    me = lax.axis_index("role")
    tp = lax.axis_index("tp")
    chip, core = me // 2, me % 2
    z, yh = chip // 2, chip % 2
    yl, xx = tp // 4, tp % 4
    sib = 2 * chip + (1 - core)

    def chip_at(dz, dy):
        return ((z + dz) % 4) * 2 + (yh + dy) % 2

    c_y, c_p, c_m, c_2 = chip_at(0, 1), chip_at(1, 0), chip_at(3, 0), chip_at(2, 0)
    c_yp, c_ym, c_y2 = chip_at(1, 1), chip_at(3, 1), chip_at(2, 1)

    def rc(src, dst, ss, rs, role, t=None):
        return pltpu.make_async_remote_copy(
            src_ref=src,
            dst_ref=dst,
            send_sem=ss,
            recv_sem=rs,
            device_id=(role, tp if t is None else t),
            device_id_type=MESH,
        )

    class Gather:
        def __init__(self, block, ss, rs):
            self.block, self.ss, self.rs = block, ss, rs

        def copy(self, i, of, to):
            return rc(self.block(of), self.block(of), self.ss(i), self.rs(of), to)

        def ops(self):
            ch = lambda c: 2 * c + core
            return [
                (me, ch(c_y)),
                (me, ch(c_p)),
                (me, ch(c_m)),
                (me, ch(c_2)),
                (me, sib),
                (ch(c_y), ch(c_p)),
                (ch(c_y), ch(c_m)),
                (ch(c_2), ch(c_y)),
            ] + [(ch(c), sib) for c in (c_p, c_m, c_y, c_2, c_yp, c_ym, c_y2)]

        def start(self, *which):
            ops = self.ops()
            for i in which:
                self.copy(i, *ops[i]).start()

        def wait(self, role):
            self.copy(0, role, sib).wait_recv()

        def first(self):
            self.start(0, 1, 2, 3, 4)

        def relay(self):
            self.wait(2 * c_y + core)
            self.start(5, 6, 10)
            self.wait(2 * c_2 + core)
            self.start(7, 11)
            self.wait(2 * c_p + core)
            self.start(8)
            self.wait(2 * c_m + core)
            self.start(9)

        def late(self):
            for i, c in ((12, c_yp), (13, c_ym), (14, c_y2)):
                self.wait(2 * c + core)
                self.start(i)

        def from_sib(self, c):
            self.wait(2 * c + (1 - core))

        def drain(self):
            ops = self.ops()
            for i in range(15):
                self.copy(i, *ops[i]).wait_send()

    def x_copy(c):
        return pltpu.make_async_copy(
            x_hbm.at[:, pl.ds(pl.multiple_of(c * 2 * KB, 2 * KB), 2 * KB)], xv.at[c], x_sem.at[c]
        )

    w_c = pltpu.make_async_copy(w_hbm, wraw, in_sem.at[0])
    kv_c = pltpu.make_async_copy(kv_hbm, kv, in_sem.at[1])
    dq_c = pltpu.make_async_copy(dq_hbm, dq, in_sem.at[2])
    dkv_c = pltpu.make_async_copy(dkv_hbm, dkv, in_sem.at[3])
    wout_c = pltpu.make_async_copy(wout_hbm, wout, in_sem.at[4])
    w_c.start()
    dq_c.start()
    dkv_c.start()
    kv_c.start()

    barrier = pltpu.get_barrier_semaphore()

    def greet_role(d, _):
        pl.semaphore_signal(barrier, inc=1, device_id=((me + d) % NR, tp), device_id_type=MESH)
        return 0

    lax.fori_loop(1, NR, greet_role, 0)
    for d in range(1, 4):
        pl.semaphore_signal(barrier, inc=1, device_id=(me, 4 * yl + (xx + d) % 4), device_id_type=MESH)
    pl.semaphore_signal(barrier, inc=1, device_id=(me, 4 * (1 - yl) + xx), device_id_type=MESH)

    chips = (chip, c_p, c_m, c_y, c_2, c_yp, c_ym, c_y2)
    for c in chips:
        x_copy(c).start()
    wout_c.start()

    lane = lax.broadcasted_iota(jnp.int32, (8, 128), 1)
    owners = [owner_ref[0, i] for i in range(NP)]
    tags = jnp.full((8, 128), -1, jnp.int32)
    slots = []
    for i in range(NP):
        rank = jnp.int32(0)
        for j in range(i):
            rank = rank + (owners[j] == owners[i]).astype(jnp.int32)
        slot = 2 * owners[i] + rank
        slots.append(slot)
        slot_of[i] = slot
        tags = jnp.where(lane == slot, req_ref[i], tags)
    vtag[...] = tags
    rtag[me] = tags

    w_c.wait()
    eye = lax.broadcasted_iota(jnp.int32, (128, 128), 0) == lax.broadcasted_iota(jnp.int32, (128, 128), 1)
    gain = gain_ref[me].astype(F32)
    for i in range(KB // 128):
        g = jnp.broadcast_to(gain[i : i + 1, :], (128, 128))
        g = jnp.sum(jnp.where(eye, g, 0.0), axis=1, keepdims=True)
        rows = slice(128 * i, 128 * i + 128)
        wv[me, rows, :] = (wraw[rows, :].astype(F32) * g).astype(BF)

    dq_c.wait()
    for s in range(STEPS):
        for h in range(PER):
            qf[pl.ds(s * PER + h, RQ, stride=RQ), :] = dq[s, :, h * HS : (h + 1) * HS].astype(F32)

    def by_request(r, _):
        qb[r] = qf[pl.ds(pl.multiple_of(r * RQ, RQ), RQ), :].astype(BF)
        return 0

    lax.fori_loop(0, RQ, by_request, 0, unroll=4)

    pl.semaphore_wait(barrier, NR - 1 + 4)

    def send_tag(d, _):
        p = (me + d) % NR
        rc(vtag, rtag.at[me], tag_ss.at[d], tag_rs.at[me], p).start()
        return 0

    lax.fori_loop(1, NR, send_tag, 0)
    w_all = Gather(lambda r: wv.at[r], lambda i: w_ss.at[i], lambda r: w_rs.at[r])
    w_all.first()

    def find_page(s, _):
        i = jnp.int32(0)
        for j in range(NP):
            i = jnp.where(slots[j] == s, j, i)
        page_of[s] = i
        return 0

    lax.fori_loop(0, 2 * NR, find_page, 0)

    acc[...] = jnp.zeros_like(acc)
    sq[...] = jnp.zeros_like(sq)

    dkv_c.wait()
    kv_c.wait()

    def attend(r, _):
        q = qb[r]
        pages = [kv[bt_ref[j, r]] for j in range(4)]
        own = dkv[...]
        keys = jnp.concatenate([p[:, :HS] for p in pages], axis=0)
        values = jnp.concatenate([p[:, HS:] for p in pages], axis=0)
        s1 = lax.dot_general(q, keys, NT_DIMS, preferred_element_type=F32) * SCALING
        s2 = lax.dot_general(q, own[:, :HS], NT_DIMS, preferred_element_type=F32) * SCALING
        col = lax.broadcasted_iota(jnp.int32, s1.shape, 1)
        s1 = jnp.where(col < len_ref[r], s1, LOW)
        col2 = lax.broadcasted_iota(jnp.int32, s2.shape, 1)
        row2 = lax.broadcasted_iota(jnp.int32, s2.shape, 0)
        s2 = jnp.where((col2 % RQ == r) & (col2 // RQ <= row2 // PER), s2, LOW)
        top = jnp.maximum(jnp.max(s1, axis=1, keepdims=True), jnp.max(s2, axis=1, keepdims=True))
        p1 = jnp.exp(s1 - top)
        p2 = jnp.exp(s2 - top)
        total = jnp.sum(p1, axis=1, keepdims=True) + jnp.sum(p2, axis=1, keepdims=True)
        o = jnp.dot(p1.astype(BF), values, preferred_element_type=F32)
        o = o + jnp.dot(p2.astype(BF), own[:, HS:], preferred_element_type=F32)
        ac[pl.ds(r, RQ, stride=RQ), :] = o / total
        lc[pl.ds(r, RQ, stride=RQ), :] = jnp.broadcast_to(top + jnp.log(total), (RQ, HS))
        return 0

    lax.fori_loop(0, RQ // 2, attend, 0, unroll=UNROLL)

    tmat = jnp.full((8, 128), -1, jnp.int32)

    def wait_tag(d, t):
        p = (me - d + NR) % NR

        @pl.when(d > 0)
        def _():
            rc(vtag, rtag.at[p], tag_ss.at[0], tag_rs.at[p], p).wait_recv()

        moved = pltpu.roll(rtag[p], (2 * p - 2 * me + 128) % 128, 1)
        return jnp.where(lane // 2 == p, moved, t)

    tmat = lax.fori_loop(0, NR, wait_tag, tmat)
    tvec[...] = tmat
    t_c = pltpu.make_async_copy(tvec, tsm, t_sem)
    t_c.start()
    t_c.wait()

    def pick(s, _):
        qs[s] = qb[jnp.maximum(tsm[0, s], 0)]
        return 0

    lax.fori_loop(0, 2 * NR, pick, 0, unroll=4)

    def send_q(d, _):
        p = (me + d) % NR
        rc(qs.at[pl.ds(2 * p, 2)], qr.at[pl.ds(2 * me, 2)], q_ss.at[d], q_rs.at[me], p).start()
        return 0

    lax.fori_loop(1, NR, send_q, 0)
    qr[pl.ds(2 * me, 2)] = qs[pl.ds(2 * me, 2)]

    w_all.relay()
    lax.fori_loop(RQ // 2, RQ, attend, 0, unroll=UNROLL)

    def project(c):
        x_copy(c).wait()

        def tile(t, _):
            rows = pl.ds(pl.multiple_of(t * TILE, TILE), TILE)
            xa = xv[c, rows, :]
            acc[rows, :] += jnp.dot(xa, wv[pl.ds(2 * c, 2)].reshape(2 * KB, KVW), preferred_element_type=F32)
            part = sq[rows, :]
            for i in range(2 * KB // 128):
                xf = xa[:, i * 128 : i * 128 + 128].astype(F32)
                part = part + xf * xf
            sq[rows, :] = part
            return 0

        lax.fori_loop(0, ROWS // TILE, tile, 0)

    w_all.wait(sib)
    project(chip)
    for c in (c_p, c_m, c_y, c_2):
        w_all.from_sib(c)
        project(c)
    w_all.late()
    for c in (c_yp, c_ym, c_y2):
        w_all.from_sib(c)
        project(c)

    def wait_q(d, _):
        p = (me - d + NR) % NR
        rc(qs.at[pl.ds(0, 2)], qr.at[pl.ds(2 * p, 2)], q_ss.at[0], q_rs.at[p], p).wait_recv()
        return 0

    lax.fori_loop(1, NR, wait_q, 0)
    bias = bias_ref[...].astype(F32)
    bias = jnp.concatenate([bias[0:1], bias[1:2]], axis=1)
    lane_k = lax.broadcasted_iota(jnp.int32, (RQ, 128), 1)

    def page(i, st):
        rows = pl.ds(pl.multiple_of(i * PAGE, PAGE), PAGE)
        inverse = lax.rsqrt(jnp.sum(sq[rows, :], axis=1, keepdims=True) * (1.0 / (NR * KB)) + EPSILON)
        f = (acc[rows, :] * inverse + bias).astype(BF)
        slot = slot_of[i]
        q = qr[slot]
        s = lax.dot_general(q, f[:, :HS], NT_DIMS, preferred_element_type=F32) * SCALING
        top = jnp.max(s, axis=1, keepdims=True)
        p = jnp.exp(s - top)
        total = jnp.sum(p, axis=1, keepdims=True)
        o = jnp.dot(p.astype(BF), f[:, HS:], preferred_element_type=F32) / total
        pacc[i] = o.astype(BF)
        return jnp.where(lane_k == slot, top + jnp.log(total), st)

    st = lax.fori_loop(0, NP, page, jnp.full((RQ, 128), LOW, F32), unroll=True)
    packed = st[0:8]
    for a in range(1, 4):
        packed = jnp.where(lane // 32 == a, pltpu.roll(st[8 * a : 8 * a + 8], 32 * a, 1), packed)
    sst[...] = packed
    rst[me] = packed

    def place(s, _):
        accs[s] = pacc[page_of[s]]
        return 0

    lax.fori_loop(0, 2 * NR, place, 0, unroll=4)

    def send_acc(d, _):
        p = (me + d) % NR
        rc(accs.at[pl.ds(2 * p, 2)], racc.at[pl.ds(2 * me, 2)], a_ss.at[d], a_rs.at[me], p).start()
        rc(sst, rst.at[me], l_ss.at[d], l_rs.at[me], p).start()
        return 0

    lax.fori_loop(1, NR, send_acc, 0)
    racc[pl.ds(2 * me, 2)] = accs[pl.ds(2 * me, 2)]

    lt[...] = jnp.full((RQ, 128), LOW, F32)

    def wait_acc(d, _):
        p = (me - d + NR) % NR
        rc(sst, rst.at[p], l_ss.at[0], l_rs.at[p], p).wait_recv()
        rc(accs.at[pl.ds(0, 2)], racc.at[pl.ds(2 * p, 2)], a_ss.at[0], a_rs.at[p], p).wait_recv()
        return 0

    lax.fori_loop(1, NR, wait_acc, 0)

    def take(p, _):
        got = rst[p]
        for a in range(4):
            moved = pltpu.roll(got, (2 * p - 2 * me - 32 * a + 256) % 128, 1)
            lt[8 * a : 8 * a + 8, :] = jnp.where(lane // 2 == p, moved, lt[8 * a : 8 * a + 8, :])
        for c in range(2):
            sb[pl.ds(2 * p + c, RQ, stride=RQ), :] = racc[2 * p + c].astype(F32)
        return 0

    lax.fori_loop(0, NR, take, 0, unroll=4)

    mine = jnp.broadcast_to(tvec[0:1, :], (RQ, 128)) == lax.broadcasted_iota(jnp.int32, (RQ, 128), 0)

    def outputs(s):
        return Gather(lambda r: aall.at[s, r], lambda i: g_ss.at[s, i], lambda r: g_rs.at[s, r])

    def merge(s):
        for h in range(PER):
            k = s * PER + h
            rows = pl.ds(pl.multiple_of(k * RQ, RQ), RQ)
            scores = jnp.where(mine, jnp.broadcast_to(lt[pl.ds(k, 1), :], (RQ, 128)), LOW)
            base = lc[rows, :]
            top = jnp.maximum(jnp.max(scores, axis=1, keepdims=True), base)
            e = jnp.exp(scores - top)
            wc = jnp.exp(base - top)
            total = wc + jnp.sum(e, axis=1, keepdims=True)
            pv = jnp.dot(e[:, : 2 * NR].astype(BF), sb[rows, :].astype(BF), preferred_element_type=F32)
            merged = (wc * ac[rows, :] + pv) / total
            aall[s, me, :, h * HS : (h + 1) * HS] = merged.astype(BF)
        outputs(s).first()

    def x_send(s, d):
        to = (xx + d) % 4
        return rc(ps.at[s, to], px.at[s, xx], p_ss.at[s, d], p_rs.at[s, xx], me, 4 * yl + to)

    def x_wait(s, d):
        of = (xx + d) % 4
        rc(ps.at[s, 0], px.at[s, of], p_ss.at[s, 0], p_rs.at[s, of], me, 4 * yl + of).wait_recv()

    def y_send(s):
        return rc(ys.at[s], py.at[s], y_ss.at[s], y_rs.at[s], me, 4 * (1 - yl) + xx)

    def product(s):
        g = outputs(s)
        g.late()
        g.wait(sib)
        for c in chips[1:]:
            g.from_sib(c)

        def part(j, _):
            a = aall[s, pl.ds(j * 8, 8)].reshape(8 * RQ, 1024)
            o = jnp.dot(a, wout[...], preferred_element_type=F32).astype(BF)
            o = o.reshape(4, 2 * RQ, NOUT)
            for i in range(4):
                ps[s, i, j] = o[i]
            return 0

        lax.fori_loop(0, 2, part, 0)
        for d in range(1, 4):
            x_send(s, d).start()

    def add_x(s):
        for d in range(1, 4):
            x_wait(s, d)
        for half in range(2):
            o = ps[s, xx, half].astype(F32)
            for d in range(1, 4):
                o = o + px[s, (xx + d) % 4, half].astype(F32)

            @pl.when(yl == half)
            def _():
                ko[s] = o

            @pl.when(yl != half)
            def _():
                ys[s] = o.astype(BF)

        y_send(s).start()

    def add_y(s):
        y_send(s).wait_recv()
        out_ref[s] = (ko[s] + py[s].astype(F32)).astype(BF)

    merge(0)
    merge(1)
    wout_c.wait()

    def round_(i, _):
        @pl.when(i < STEPS)
        def _():
            outputs(i).relay()

        @pl.when(i < STEPS - 2)
        def _():
            merge(i + 2)

        @pl.when((i >= 1) & (i <= STEPS))
        def _():
            product(i - 1)

        @pl.when((i >= 2) & (i <= STEPS + 1))
        def _():
            add_x(i - 2)

        @pl.when(i >= 3)
        def _():
            add_y(i - 3)

        return 0

    lax.fori_loop(0, STEPS + 3, round_, 0)

    def drain(d, _):
        rc(vtag, rtag.at[me], tag_ss.at[d], tag_rs.at[me], sib).wait_send()
        rc(qs.at[pl.ds(0, 2)], qr.at[pl.ds(0, 2)], q_ss.at[d], q_rs.at[me], sib).wait_send()
        rc(accs.at[pl.ds(0, 2)], racc.at[pl.ds(0, 2)], a_ss.at[d], a_rs.at[me], sib).wait_send()
        rc(sst, rst.at[me], l_ss.at[d], l_rs.at[me], sib).wait_send()
        return 0

    lax.fori_loop(1, NR, drain, 0)
    w_all.drain()

    def drain_s(s, _):
        outputs(s).drain()
        for d in range(1, 4):
            x_send(s, d).wait_send()
        y_send(s).wait_send()
        return 0

    lax.fori_loop(0, STEPS, drain_s, 0)


def body(
    x_pre,
    ln_gain,
    w_kv,
    kv_bias,
    page_owner,
    page_req,
    kv_pool,
    block_table,
    cache_len,
    dec_q,
    dec_kv,
    w_out,
):
    any_spec = pl.BlockSpec(memory_space=pl.ANY)
    smem = pl.BlockSpec(memory_space=pltpu.SMEM)
    vmem = pl.BlockSpec(memory_space=pltpu.VMEM)
    dma = pltpu.SemaphoreType.DMA
    V = pltpu.VMEM
    scratch = [
        V((8, ROWS, 2 * KB), BF),
        V((KB, KVW), BF),
        V((NR, KB, KVW), BF),
        V((32, PAGE, KVW), BF),
        V((STEPS, RQ, 1024), BF),
        V((STEPS * RQ, KVW), BF),
        V((1024, NOUT), BF),
        V((ROWS, KVW), F32),
        V((ROWS, 128), F32),
        V((RQ * RQ, HS), F32),
        V((RQ, RQ, HS), BF),
        V((RQ * RQ, HS), F32),
        V((RQ * RQ, HS), F32),
        V((8, 128), jnp.int32),
        V((NR, 8, 128), jnp.int32),
        V((8, 128), jnp.int32),
        pltpu.SMEM((8, 128), jnp.int32),
        pltpu.SMEM((16,), jnp.int32),
        pltpu.SMEM((2 * NR,), jnp.int32),
        V((2 * NR, RQ, HS), BF),
        V((2 * NR, RQ, HS), BF),
        V((NP, RQ, HS), BF),
        V((2 * NR, RQ, HS), BF),
        V((2 * NR, RQ, HS), BF),
        V((8, 128), F32),
        V((NR, 8, 128), F32),
        V((RQ, 128), F32),
        V((RQ * RQ, HS), F32),
        V((STEPS, NR, RQ, 1024), BF),
        V((STEPS, 4, 2, 2 * RQ, NOUT), BF),
        V((STEPS, 4, 2, 2 * RQ, NOUT), BF),
        V((STEPS, 2 * RQ, NOUT), BF),
        V((STEPS, 2 * RQ, NOUT), BF),
        V((STEPS, 2 * RQ, NOUT), F32),
        dma((8,)),
        dma((5,)),
        dma,
        dma((15,)),
        dma((NR,)),
        dma((NR,)),
        dma((NR,)),
        dma((NR,)),
        dma((NR,)),
        dma((NR,)),
        dma((NR,)),
        dma((NR,)),
        dma((NR,)),
        dma((STEPS, 15)),
        dma((STEPS, NR)),
        dma((STEPS, 4)),
        dma((STEPS, 4)),
        dma((STEPS,)),
        dma((STEPS,)),
    ]
    return pl.pallas_call(
        kernel,
        out_shape=jax.ShapeDtypeStruct((STEPS, 2 * RQ, NOUT), BF),
        in_specs=[any_spec, vmem, any_spec, vmem, smem, smem, any_spec, smem, smem, any_spec, any_spec, any_spec],
        out_specs=vmem,
        scratch_shapes=scratch,
        compiler_params=pltpu.CompilerParams(
            collective_id=0, has_side_effects=True, vmem_limit_bytes=58 * 1024 * 1024
        ),
    )(
        x_pre,
        ln_gain.reshape(NR, KB // 128, 128),
        w_kv,
        kv_bias.reshape(2, HS),
        page_owner.T,
        page_req,
        kv_pool,
        block_table.T,
        cache_len,
        dec_q,
        dec_kv.reshape(STEPS * RQ, KVW),
        w_out,
    )


def solution(mesh):
    return jax.shard_map(
        body,
        mesh=mesh,
        in_specs=(
            P("role", None),
            P(),
            P("role", "tp"),
            P("tp"),
            P("role", None),
            P("role"),
            P("role", None, "tp"),
            P("role", None),
            P("role"),
            P(None, "role", "tp"),
            P(None, "role", "tp"),
            P("tp", "role"),
        ),
        out_specs=P(None, "tp", "role"),
        check_vma=False,
    )
```

```python
import functools
import math

import jax
import jax.numpy as jnp
from jax import lax
from jax.experimental import pallas as pl
from jax.experimental.pallas import tpu as pltpu
from jax.sharding import PartitionSpec as P

HS = 128
PAGE = 128
EPSILON = 1e-06
LOW = -1e30
MESH = pl.DeviceIdType.MESH
BF = jnp.bfloat16
F32 = jnp.float32

NR = 16
NT = 8
NP = 11
RQ = 32
STEPS = 4
PER = 8
KB = 512
KVW = 256
ROWS = NP * PAGE
TILE = 704
UNROLL = 4
NOUT = 512
SCALING = 1.0 / math.sqrt(HS)
NT_DIMS = (((1,), (1,)), ((), ()))


def kernel(
    x_hbm,
    gain_ref,
    w_hbm,
    bias_ref,
    owner_ref,
    req_ref,
    kv_hbm,
    bt_ref,
    len_ref,
    dq_hbm,
    dkv_hbm,
    wout_hbm,
    out_ref,
    xv,
    wraw,
    wv,
    kv,
    dq,
    dkv,
    wout,
    acc,
    sq,
    qf,
    qb,
    ac,
    lc,
    vtag,
    rtag,
    tvec,
    tsm,
    slot_of,
    page_of,
    qs,
    qr,
    pacc,
    accs,
    racc,
    sst,
    rst,
    lt,
    sb,
    aall,
    ps,
    pa,
    px,
    ys,
    py,
    ko,
    x_sem,
    in_sem,
    t_sem,
    w_ss,
    w_rs,
    tag_ss,
    tag_rs,
    q_ss,
    q_rs,
    a_ss,
    a_rs,
    l_ss,
    l_rs,
    g_ss,
    g_rs,
    p_ss,
    p_rs,
    y_ss,
    y_rs,
):
    me = lax.axis_index("role")
    tp = lax.axis_index("tp")
    chip, core = me // 2, me % 2
    z, yh = chip // 2, chip % 2
    yl, xx = tp // 4, tp % 4
    sib = 2 * chip + (1 - core)

    def chip_at(dz, dy):
        return ((z + dz) % 4) * 2 + (yh + dy) % 2

    c_y, c_p, c_m, c_2 = chip_at(0, 1), chip_at(1, 0), chip_at(3, 0), chip_at(2, 0)
    c_yp, c_ym, c_y2 = chip_at(1, 1), chip_at(3, 1), chip_at(2, 1)

    def rc(src, dst, ss, rs, role, t=None):
        return pltpu.make_async_remote_copy(
            src_ref=src,
            dst_ref=dst,
            send_sem=ss,
            recv_sem=rs,
            device_id=(role, tp if t is None else t),
            device_id_type=MESH,
        )

    class Gather:
        def __init__(self, block, ss, rs):
            self.block, self.ss, self.rs = block, ss, rs

        def copy(self, i, of, to):
            return rc(self.block(of), self.block(of), self.ss(i), self.rs(of), to)

        def ops(self):
            ch = lambda c: 2 * c + core
            return [
                (me, ch(c_y)),
                (me, ch(c_p)),
                (me, ch(c_m)),
                (me, ch(c_2)),
                (me, sib),
                (ch(c_y), ch(c_p)),
                (ch(c_y), ch(c_m)),
                (ch(c_2), ch(c_y)),
            ] + [(ch(c), sib) for c in (c_p, c_m, c_y, c_2, c_yp, c_ym, c_y2)]

        def start(self, *which):
            ops = self.ops()
            for i in which:
                self.copy(i, *ops[i]).start()

        def wait(self, role):
            self.copy(0, role, sib).wait_recv()

        def first(self):
            self.start(0, 1, 2, 3, 4)

        def relay_near(self):
            self.wait(2 * c_y + core)
            self.start(5, 6, 10)
            self.wait(2 * c_p + core)
            self.start(8)
            self.wait(2 * c_m + core)
            self.start(9)

        def relay_far(self):
            self.wait(2 * c_2 + core)
            self.start(7, 11)

        def late(self):
            for i, c in ((12, c_yp), (13, c_ym), (14, c_y2)):
                self.wait(2 * c + core)
                self.start(i)

        def from_sib(self, c):
            self.wait(2 * c + (1 - core))

        def drain(self):
            ops = self.ops()
            for i in range(15):
                self.copy(i, *ops[i]).wait_send()

    def x_copy(c):
        return pltpu.make_async_copy(
            x_hbm.at[:, pl.ds(pl.multiple_of(c * 2 * KB, 2 * KB), 2 * KB)], xv.at[c], x_sem.at[c]
        )

    w_c = pltpu.make_async_copy(w_hbm, wraw, in_sem.at[0])
    kv_c = pltpu.make_async_copy(kv_hbm, kv, in_sem.at[1])
    dq_c = pltpu.make_async_copy(dq_hbm, dq, in_sem.at[2])
    dkv_c = pltpu.make_async_copy(dkv_hbm, dkv, in_sem.at[3])
    wout_c = pltpu.make_async_copy(wout_hbm, wout, in_sem.at[4])
    w_c.start()
    dq_c.start()
    dkv_c.start()
    kv_c.start()

    barrier = pltpu.get_barrier_semaphore()

    def greet_role(d, _):
        pl.semaphore_signal(barrier, inc=1, device_id=((me + d) % NR, tp), device_id_type=MESH)
        return 0

    lax.fori_loop(1, NR, greet_role, 0)
    for d in (1, 3):
        pl.semaphore_signal(barrier, inc=1, device_id=(me, 4 * yl + (xx + d) % 4), device_id_type=MESH)
    pl.semaphore_signal(barrier, inc=1, device_id=(me, 4 * (1 - yl) + xx), device_id_type=MESH)

    chips = (chip, c_p, c_m, c_y, c_2, c_yp, c_ym, c_y2)
    for c in chips:
        x_copy(c).start()
    wout_c.start()

    lane = lax.broadcasted_iota(jnp.int32, (8, 128), 1)
    owners = [owner_ref[0, i] for i in range(NP)]
    tags = jnp.full((8, 128), -1, jnp.int32)
    slots = []
    for i in range(NP):
        rank = jnp.int32(0)
        for j in range(i):
            rank = rank + (owners[j] == owners[i]).astype(jnp.int32)
        slot = 2 * owners[i] + rank
        slots.append(slot)
        slot_of[i] = slot
        tags = jnp.where(lane == slot, req_ref[i], tags)
    vtag[...] = tags
    rtag[me] = tags

    w_c.wait()
    eye = lax.broadcasted_iota(jnp.int32, (128, 128), 0) == lax.broadcasted_iota(jnp.int32, (128, 128), 1)
    gain = gain_ref[me].astype(F32)
    for i in range(KB // 128):
        g = jnp.broadcast_to(gain[i : i + 1, :], (128, 128))
        g = jnp.sum(jnp.where(eye, g, 0.0), axis=1, keepdims=True)
        rows = slice(128 * i, 128 * i + 128)
        wv[me, rows, :] = (wraw[rows, :].astype(F32) * g).astype(BF)

    dq_c.wait()
    for s in range(STEPS):
        for h in range(PER):
            qf[pl.ds(s * PER + h, RQ, stride=RQ), :] = dq[s, :, h * HS : (h + 1) * HS].astype(F32)

    def by_request(r, _):
        qb[r] = qf[pl.ds(pl.multiple_of(r * RQ, RQ), RQ), :].astype(BF)
        return 0

    lax.fori_loop(0, RQ, by_request, 0, unroll=4)

    pl.semaphore_wait(barrier, NR - 1 + 3)

    def send_tag(d, _):
        p = (me + d) % NR
        rc(vtag, rtag.at[me], tag_ss.at[d], tag_rs.at[me], p).start()
        return 0

    lax.fori_loop(1, NR, send_tag, 0)
    w_all = Gather(lambda r: wv.at[r], lambda i: w_ss.at[i], lambda r: w_rs.at[r])
    w_all.first()

    def find_page(s, _):
        i = jnp.int32(0)
        for j in range(NP):
            i = jnp.where(slots[j] == s, j, i)
        page_of[s] = i
        return 0

    lax.fori_loop(0, 2 * NR, find_page, 0)

    acc[...] = jnp.zeros_like(acc)
    sq[...] = jnp.zeros_like(sq)

    dkv_c.wait()
    kv_c.wait()

    def attend(r, _):
        q = qb[r]
        pages = [kv[bt_ref[j, r]] for j in range(4)]
        own = dkv[...]
        keys = jnp.concatenate([p[:, :HS] for p in pages], axis=0)
        values = jnp.concatenate([p[:, HS:] for p in pages], axis=0)
        s1 = lax.dot_general(q, keys, NT_DIMS, preferred_element_type=F32) * SCALING
        s2 = lax.dot_general(q, own[:, :HS], NT_DIMS, preferred_element_type=F32) * SCALING
        col = lax.broadcasted_iota(jnp.int32, s1.shape, 1)
        s1 = jnp.where(col < len_ref[r], s1, LOW)
        col2 = lax.broadcasted_iota(jnp.int32, s2.shape, 1)
        row2 = lax.broadcasted_iota(jnp.int32, s2.shape, 0)
        s2 = jnp.where((col2 % RQ == r) & (col2 // RQ <= row2 // PER), s2, LOW)
        top = jnp.maximum(jnp.max(s1, axis=1, keepdims=True), jnp.max(s2, axis=1, keepdims=True))
        p1 = jnp.exp(s1 - top)
        p2 = jnp.exp(s2 - top)
        total = jnp.sum(p1, axis=1, keepdims=True) + jnp.sum(p2, axis=1, keepdims=True)
        o = jnp.dot(p1.astype(BF), values, preferred_element_type=F32)
        o = o + jnp.dot(p2.astype(BF), own[:, HS:], preferred_element_type=F32)
        ac[pl.ds(r, RQ, stride=RQ), :] = o / total
        lc[pl.ds(r, RQ, stride=RQ), :] = jnp.broadcast_to(top + jnp.log(total), (RQ, HS))
        return 0

    def ask():
        tmat = jnp.full((8, 128), -1, jnp.int32)

        def wait_tag(d, t):
            p = (me - d + NR) % NR

            @pl.when(d > 0)
            def _():
                rc(vtag, rtag.at[p], tag_ss.at[0], tag_rs.at[p], p).wait_recv()

            moved = pltpu.roll(rtag[p], (2 * p - 2 * me + 128) % 128, 1)
            return jnp.where(lane // 2 == p, moved, t)

        tmat = lax.fori_loop(0, NR, wait_tag, tmat)
        tvec[...] = tmat
        t_c = pltpu.make_async_copy(tvec, tsm, t_sem)
        t_c.start()
        t_c.wait()

        def pick(s, _):
            qs[s] = qb[jnp.maximum(tsm[0, s], 0)]
            return 0

        lax.fori_loop(0, 2 * NR, pick, 0, unroll=4)

        def send_q(d, _):
            p = (me + d) % NR
            rc(qs.at[pl.ds(2 * p, 2)], qr.at[pl.ds(2 * me, 2)], q_ss.at[d], q_rs.at[me], p).start()
            return 0

        lax.fori_loop(1, NR, send_q, 0)
        qr[pl.ds(2 * me, 2)] = qs[pl.ds(2 * me, 2)]

    def project(c):
        x_copy(c).wait()

        def tile(t, _):
            rows = pl.ds(pl.multiple_of(t * TILE, TILE), TILE)
            xa = xv[c, rows, :]
            acc[rows, :] += jnp.dot(xa, wv[pl.ds(2 * c, 2)].reshape(2 * KB, KVW), preferred_element_type=F32)
            part = sq[rows, :]
            for i in range(2 * KB // 128):
                xf = xa[:, i * 128 : i * 128 + 128].astype(F32)
                part = part + xf * xf
            sq[rows, :] = part
            return 0

        lax.fori_loop(0, ROWS // TILE, tile, 0)

    def group(i, _):
        lax.fori_loop(0, 8, lambda r, carry: attend(8 * i + r, carry), 0, unroll=UNROLL)

        @pl.when(i == 1)
        def _():
            ask()
            w_all.relay_near()

        @pl.when(i == 2)
        def _():
            w_all.wait(sib)
            project(chip)
            w_all.relay_far()

        return 0

    lax.fori_loop(0, RQ // 8, group, 0)

    def next_chip(i, _):
        c = chip_at(i % 4, i // 4)
        w_all.from_sib(c)
        project(c)
        return 0

    lax.fori_loop(1, 5, next_chip, 0)
    w_all.late()
    lax.fori_loop(5, 8, next_chip, 0)

    def wait_q(d, _):
        p = (me - d + NR) % NR
        rc(qs.at[pl.ds(0, 2)], qr.at[pl.ds(2 * p, 2)], q_ss.at[0], q_rs.at[p], p).wait_recv()
        return 0

    lax.fori_loop(1, NR, wait_q, 0)
    bias = bias_ref[...].astype(F32)
    bias = jnp.concatenate([bias[0:1], bias[1:2]], axis=1)
    lane_k = lax.broadcasted_iota(jnp.int32, (RQ, 128), 1)

    def page(i, st):
        rows = pl.ds(pl.multiple_of(i * PAGE, PAGE), PAGE)
        inverse = lax.rsqrt(jnp.sum(sq[rows, :], axis=1, keepdims=True) * (1.0 / (NR * KB)) + EPSILON)
        f = (acc[rows, :] * inverse + bias).astype(BF)
        slot = slot_of[i]
        q = qr[slot]
        s = lax.dot_general(q, f[:, :HS], NT_DIMS, preferred_element_type=F32) * SCALING
        top = jnp.max(s, axis=1, keepdims=True)
        p = jnp.exp(s - top)
        total = jnp.sum(p, axis=1, keepdims=True)
        o = jnp.dot(p.astype(BF), f[:, HS:], preferred_element_type=F32) / total
        pacc[i] = o.astype(BF)
        return jnp.where(lane_k == slot, top + jnp.log(total), st)

    st = lax.fori_loop(0, NP, page, jnp.full((RQ, 128), LOW, F32), unroll=True)
    packed = st[0:8]
    for a in range(1, 4):
        packed = jnp.where(lane // 32 == a, pltpu.roll(st[8 * a : 8 * a + 8], 32 * a, 1), packed)
    sst[...] = packed
    rst[me] = packed

    def place(s, _):
        accs[s] = pacc[page_of[s]]
        return 0

    lax.fori_loop(0, 2 * NR, place, 0, unroll=4)

    def send_acc(d, _):
        p = (me + d) % NR
        rc(accs.at[pl.ds(2 * p, 2)], racc.at[pl.ds(2 * me, 2)], a_ss.at[d], a_rs.at[me], p).start()
        rc(sst, rst.at[me], l_ss.at[d], l_rs.at[me], p).start()
        return 0

    lax.fori_loop(1, NR, send_acc, 0)
    racc[pl.ds(2 * me, 2)] = accs[pl.ds(2 * me, 2)]

    lt[...] = jnp.full((RQ, 128), LOW, F32)

    def wait_acc(d, _):
        p = (me - d + NR) % NR
        rc(sst, rst.at[p], l_ss.at[0], l_rs.at[p], p).wait_recv()
        rc(accs.at[pl.ds(0, 2)], racc.at[pl.ds(2 * p, 2)], a_ss.at[0], a_rs.at[p], p).wait_recv()
        return 0

    lax.fori_loop(1, NR, wait_acc, 0)

    def take(p, _):
        got = rst[p]
        for a in range(4):
            moved = pltpu.roll(got, (2 * p - 2 * me - 32 * a + 256) % 128, 1)
            lt[8 * a : 8 * a + 8, :] = jnp.where(lane // 2 == p, moved, lt[8 * a : 8 * a + 8, :])
        for c in range(2):
            sb[pl.ds(2 * p + c, RQ, stride=RQ), :] = racc[2 * p + c].astype(F32)
        return 0

    lax.fori_loop(0, NR, take, 0, unroll=4)

    mine = jnp.broadcast_to(tvec[0:1, :], (RQ, 128)) == lax.broadcasted_iota(jnp.int32, (RQ, 128), 0)

    def outputs(s):
        return Gather(lambda r: aall.at[s, r], lambda i: g_ss.at[s, i], lambda r: g_rs.at[s, r])

    def merge(s):
        for h in range(PER):
            k = s * PER + h
            rows = pl.ds(pl.multiple_of(k * RQ, RQ), RQ)
            scores = jnp.where(mine, jnp.broadcast_to(lt[pl.ds(k, 1), :], (RQ, 128)), LOW)
            base = lc[rows, :]
            top = jnp.maximum(jnp.max(scores, axis=1, keepdims=True), base)
            e = jnp.exp(scores - top)
            wc = jnp.exp(base - top)
            total = wc + jnp.sum(e, axis=1, keepdims=True)
            pv = jnp.dot(e[:, : 2 * NR].astype(BF), sb[rows, :].astype(BF), preferred_element_type=F32)
            merged = (wc * ac[rows, :] + pv) / total
            aall[s, me, :, h * HS : (h + 1) * HS] = merged.astype(BF)
        outputs(s).first()

    x_p, x_m, x_2 = (xx + 1) % 4, (xx + 3) % 4, (xx + 2) % 4

    def x_send(s, i):
        to = x_m if i % 2 else x_p
        src, dst = (
            (ps.at[s, x_2, 0], pa.at[s, 0]),
            (ps.at[s, x_2, 1], pa.at[s, 1]),
            (ps.at[s, x_p, 1], px.at[s, 0, 1]),
            (ps.at[s, x_m, 0], px.at[s, 1, 0]),
            (ps.at[s, x_p, 0], px.at[s, 0, 0]),
            (ps.at[s, x_m, 1], px.at[s, 1, 1]),
        )[i]
        return rc(src, dst, p_ss.at[s, i], p_rs.at[s, i], me, 4 * yl + to)

    def relay_x(s):
        x_send(s, 0).wait_recv()
        ps[s, x_p, 0] = (ps[s, x_p, 0].astype(F32) + pa[s, 0].astype(F32)).astype(BF)
        x_send(s, 4).start()
        x_send(s, 1).wait_recv()
        ps[s, x_m, 1] = (ps[s, x_m, 1].astype(F32) + pa[s, 1].astype(F32)).astype(BF)
        x_send(s, 5).start()

    def y_send(s):
        return rc(ys.at[s], py.at[s], y_ss.at[s], y_rs.at[s], me, 4 * (1 - yl) + xx)

    def product(s):
        g = outputs(s)
        g.late()
        g.wait(sib)
        for c in chips[1:]:
            g.from_sib(c)

        def part(j, _):
            a = aall[s, pl.ds(j * 8, 8)].reshape(8 * RQ, 1024)
            o = jnp.dot(a, wout[...], preferred_element_type=F32).astype(BF)
            o = o.reshape(4, 2 * RQ, NOUT)
            for i in range(4):
                for h in range(2):
                    ps[s, i, h, j] = o[i, :, h * 256 : h * 256 + 256]
            return 0

        lax.fori_loop(0, 2, part, 0)
        for i in range(4):
            x_send(s, i).start()

    def add_x(s):
        for i in range(2, 6):
            x_send(s, i).wait_recv()
        for half in range(2):
            o = jnp.concatenate(
                [
                    ps[s, xx, h, half].astype(F32) + px[s, 0, h, half].astype(F32) + px[s, 1, h, half].astype(F32)
                    for h in range(2)
                ],
                axis=1,
            )

            @pl.when(yl == half)
            def _():
                ko[s] = o

            @pl.when(yl != half)
            def _():
                ys[s] = o.astype(BF)

        y_send(s).start()

    def add_y(s):
        y_send(s).wait_recv()
        out_ref[s] = (ko[s] + py[s].astype(F32)).astype(BF)

    merge(0)
    merge(1)
    wout_c.wait()

    def round_(i, _):
        @pl.when(i < STEPS)
        def _():
            outputs(i).relay_near()
            outputs(i).relay_far()

        @pl.when(i < STEPS - 2)
        def _():
            merge(i + 2)

        @pl.when((i >= 1) & (i <= STEPS))
        def _():
            product(i - 1)

        @pl.when((i >= 2) & (i <= STEPS + 1))
        def _():
            relay_x(i - 2)

        @pl.when((i >= 3) & (i <= STEPS + 2))
        def _():
            add_x(i - 3)

        @pl.when(i >= 4)
        def _():
            add_y(i - 4)

        return 0

    lax.fori_loop(0, STEPS + 4, round_, 0)

    def drain(d, _):
        rc(vtag, rtag.at[me], tag_ss.at[d], tag_rs.at[me], sib).wait_send()
        rc(qs.at[pl.ds(0, 2)], qr.at[pl.ds(0, 2)], q_ss.at[d], q_rs.at[me], sib).wait_send()
        rc(accs.at[pl.ds(0, 2)], racc.at[pl.ds(0, 2)], a_ss.at[d], a_rs.at[me], sib).wait_send()
        rc(sst, rst.at[me], l_ss.at[d], l_rs.at[me], sib).wait_send()
        return 0

    lax.fori_loop(1, NR, drain, 0)
    w_all.drain()

    def drain_s(s, _):
        outputs(s).drain()
        for i in range(6):
            x_send(s, i).wait_send()
        y_send(s).wait_send()
        return 0

    lax.fori_loop(0, STEPS, drain_s, 0)


def body(
    x_pre,
    ln_gain,
    w_kv,
    kv_bias,
    page_owner,
    page_req,
    kv_pool,
    block_table,
    cache_len,
    dec_q,
    dec_kv,
    w_out,
):
    any_spec = pl.BlockSpec(memory_space=pl.ANY)
    smem = pl.BlockSpec(memory_space=pltpu.SMEM)
    vmem = pl.BlockSpec(memory_space=pltpu.VMEM)
    dma = pltpu.SemaphoreType.DMA
    V = pltpu.VMEM
    scratch = [
        V((8, ROWS, 2 * KB), BF),
        V((KB, KVW), BF),
        V((NR, KB, KVW), BF),
        V((32, PAGE, KVW), BF),
        V((STEPS, RQ, 1024), BF),
        V((STEPS * RQ, KVW), BF),
        V((1024, NOUT), BF),
        V((ROWS, KVW), F32),
        V((ROWS, 128), F32),
        V((RQ * RQ, HS), F32),
        V((RQ, RQ, HS), BF),
        V((RQ * RQ, HS), F32),
        V((RQ * RQ, HS), F32),
        V((8, 128), jnp.int32),
        V((NR, 8, 128), jnp.int32),
        V((8, 128), jnp.int32),
        pltpu.SMEM((8, 128), jnp.int32),
        pltpu.SMEM((16,), jnp.int32),
        pltpu.SMEM((2 * NR,), jnp.int32),
        V((2 * NR, RQ, HS), BF),
        V((2 * NR, RQ, HS), BF),
        V((NP, RQ, HS), BF),
        V((2 * NR, RQ, HS), BF),
        V((2 * NR, RQ, HS), BF),
        V((8, 128), F32),
        V((NR, 8, 128), F32),
        V((RQ, 128), F32),
        V((RQ * RQ, HS), F32),
        V((STEPS, NR, RQ, 1024), BF),
        V((STEPS, 4, 2, 2, 2 * RQ, 256), BF),
        V((STEPS, 2, 2, 2 * RQ, 256), BF),
        V((STEPS, 2, 2, 2, 2 * RQ, 256), BF),
        V((STEPS, 2 * RQ, NOUT), BF),
        V((STEPS, 2 * RQ, NOUT), BF),
        V((STEPS, 2 * RQ, NOUT), F32),
        dma((8,)),
        dma((5,)),
        dma,
        dma((15,)),
        dma((NR,)),
        dma((NR,)),
        dma((NR,)),
        dma((NR,)),
        dma((NR,)),
        dma((NR,)),
        dma((NR,)),
        dma((NR,)),
        dma((NR,)),
        dma((STEPS, 15)),
        dma((STEPS, NR)),
        dma((STEPS, 6)),
        dma((STEPS, 6)),
        dma((STEPS,)),
        dma((STEPS,)),
    ]
    return pl.pallas_call(
        kernel,
        out_shape=jax.ShapeDtypeStruct((STEPS, 2 * RQ, NOUT), BF),
        in_specs=[any_spec, vmem, any_spec, vmem, smem, smem, any_spec, smem, smem, any_spec, any_spec, any_spec],
        out_specs=vmem,
        scratch_shapes=scratch,
        compiler_params=pltpu.CompilerParams(
            collective_id=0, has_side_effects=True, vmem_limit_bytes=58 * 1024 * 1024
        ),
    )(
        x_pre,
        ln_gain.reshape(NR, KB // 128, 128),
        w_kv,
        kv_bias.reshape(2, HS),
        page_owner.T,
        page_req,
        kv_pool,
        block_table.T,
        cache_len,
        dec_q,
        dec_kv.reshape(STEPS * RQ, KVW),
        w_out,
    )


def solution(mesh):
    return jax.shard_map(
        body,
        mesh=mesh,
        in_specs=(
            P("role", None),
            P(),
            P("role", "tp"),
            P("tp"),
            P("role", None),
            P("role"),
            P("role", None, "tp"),
            P("role", None),
            P("role"),
            P(None, "role", "tp"),
            P(None, "role", "tp"),
            P("tp", "role"),
        ),
        out_specs=P(None, "tp", "role"),
        check_vma=False,
    )
```

```python
import functools
import math

import jax
import jax.numpy as jnp
from jax import lax
from jax.experimental import pallas as pl
from jax.experimental.pallas import tpu as pltpu
from jax.sharding import PartitionSpec as P

HS = 128
PAGE = 128
EPSILON = 1e-06
LOW = -1e30
MESH = pl.DeviceIdType.MESH
BF = jnp.bfloat16
F32 = jnp.float32

NR = 16
NT = 8
NP = 11
RQ = 32
STEPS = 4
PER = 8
KB = 512
KVW = 256
ROWS = NP * PAGE
TILE = 704
SQ_TILE = 176
UNROLL = 4
NOUT = 512
SCALING = 1.0 / math.sqrt(HS)
NT_DIMS = (((1,), (1,)), ((), ()))


def kernel(
    x_hbm,
    gain_ref,
    w_hbm,
    bias_ref,
    owner_ref,
    req_ref,
    kv_hbm,
    bt_ref,
    len_ref,
    dq_hbm,
    dkv_hbm,
    wout_hbm,
    out_ref,
    xv,
    wv,
    kv,
    dq,
    dkv,
    wout,
    acc,
    sq,
    qf,
    qb,
    ac,
    lc,
    vtag,
    rtag,
    tvec,
    tsm,
    slot_of,
    page_of,
    qs,
    qr,
    pacc,
    accs,
    racc,
    sst,
    rst,
    lt,
    sb,
    aall,
    ps,
    pa,
    px,
    ys,
    py,
    ko,
    x_sem,
    in_sem,
    t_sem,
    w_ss,
    w_rs,
    tag_ss,
    tag_rs,
    q_ss,
    q_rs,
    a_ss,
    a_rs,
    l_ss,
    l_rs,
    g_ss,
    g_rs,
    p_ss,
    p_rs,
    y_ss,
    y_rs,
):
    me = lax.axis_index("role")
    tp = lax.axis_index("tp")
    chip, core = me // 2, me % 2
    z, yh = chip // 2, chip % 2
    yl, xx = tp // 4, tp % 4
    sib = 2 * chip + (1 - core)

    def chip_at(dz, dy):
        return ((z + dz) % 4) * 2 + (yh + dy) % 2

    c_y, c_p, c_m, c_2 = chip_at(0, 1), chip_at(1, 0), chip_at(3, 0), chip_at(2, 0)
    c_yp, c_ym, c_y2 = chip_at(1, 1), chip_at(3, 1), chip_at(2, 1)

    def rc(src, dst, ss, rs, role, t=None):
        return pltpu.make_async_remote_copy(
            src_ref=src,
            dst_ref=dst,
            send_sem=ss,
            recv_sem=rs,
            device_id=(role, tp if t is None else t),
            device_id_type=MESH,
        )

    class Gather:
        def __init__(self, block, ss, rs):
            self.block, self.ss, self.rs = block, ss, rs

        def copy(self, i, of, to):
            return rc(self.block(of), self.block(of), self.ss(i), self.rs(of), to)

        def ops(self):
            ch = lambda c: 2 * c + core
            return [
                (me, ch(c_y)),
                (me, ch(c_p)),
                (me, ch(c_m)),
                (me, ch(c_2)),
                (me, sib),
                (ch(c_y), ch(c_p)),
                (ch(c_y), ch(c_m)),
                (ch(c_2), ch(c_y)),
            ] + [(ch(c), sib) for c in (c_p, c_m, c_y, c_2, c_yp, c_ym, c_y2)]

        def start(self, *which):
            ops = self.ops()
            for i in which:
                self.copy(i, *ops[i]).start()

        def wait(self, role):
            self.copy(0, role, sib).wait_recv()

        def first(self):
            self.start(0, 1, 2, 3, 4)

        def relay_near(self):
            self.wait(2 * c_y + core)
            self.start(5, 6, 10)
            self.wait(2 * c_p + core)
            self.start(8)
            self.wait(2 * c_m + core)
            self.start(9)

        def relay_far(self):
            self.wait(2 * c_2 + core)
            self.start(7, 11)

        def late(self):
            for i, c in ((12, c_yp), (13, c_ym), (14, c_y2)):
                self.wait(2 * c + core)
                self.start(i)

        def from_sib(self, c):
            self.wait(2 * c + (1 - core))

        def drain(self):
            ops = self.ops()
            for i in range(15):
                self.copy(i, *ops[i]).wait_send()

    def x_copy(c):
        return pltpu.make_async_copy(
            x_hbm.at[:, pl.ds(pl.multiple_of(c * 2 * KB, 2 * KB), 2 * KB)], xv.at[c], x_sem.at[c]
        )

    w_c = pltpu.make_async_copy(w_hbm, wv.at[me], in_sem.at[0])
    kv_c = pltpu.make_async_copy(kv_hbm, kv, in_sem.at[1])
    dq_c = pltpu.make_async_copy(dq_hbm, dq, in_sem.at[2])
    dkv_c = pltpu.make_async_copy(dkv_hbm, dkv, in_sem.at[3])
    wout_c = pltpu.make_async_copy(wout_hbm, wout, in_sem.at[4])
    w_c.start()
    dq_c.start()
    dkv_c.start()
    kv_c.start()

    barrier = pltpu.get_barrier_semaphore()

    def greet_role(d, _):
        pl.semaphore_signal(barrier, inc=1, device_id=((me + d) % NR, tp), device_id_type=MESH)
        return 0

    lax.fori_loop(1, NR, greet_role, 0)
    for d in (1, 3):
        pl.semaphore_signal(barrier, inc=1, device_id=(me, 4 * yl + (xx + d) % 4), device_id_type=MESH)
    pl.semaphore_signal(barrier, inc=1, device_id=(me, 4 * (1 - yl) + xx), device_id_type=MESH)

    chips = [chip_at(i % 4, i // 4) for i in range(8)]
    for c in chips:
        x_copy(c).start()
    wout_c.start()

    lane = lax.broadcasted_iota(jnp.int32, (8, 128), 1)
    owners = [owner_ref[0, i] for i in range(NP)]
    tags = jnp.full((8, 128), -1, jnp.int32)
    slots = []
    for i in range(NP):
        rank = jnp.int32(0)
        for j in range(i):
            rank = rank + (owners[j] == owners[i]).astype(jnp.int32)
        slot = 2 * owners[i] + rank
        slots.append(slot)
        slot_of[i] = slot
        tags = jnp.where(lane == slot, req_ref[i], tags)
    vtag[...] = tags
    rtag[me] = tags

    dq_c.wait()
    for s in range(STEPS):
        for h in range(PER):
            qf[pl.ds(s * PER + h, RQ, stride=RQ), :] = dq[s, :, h * HS : (h + 1) * HS].astype(F32)

    def by_request(r, _):
        qb[r] = qf[pl.ds(pl.multiple_of(r * RQ, RQ), RQ), :].astype(BF)
        return 0

    lax.fori_loop(0, RQ, by_request, 0, unroll=4)

    sq[...] = jnp.zeros_like(sq)

    def squares(i, _):
        c = chip_at(i % 4, i // 4)
        x_copy(c).wait()

        def tile(t, _):
            rows = pl.ds(pl.multiple_of(t * SQ_TILE, SQ_TILE), SQ_TILE)
            part = sq[rows, :]
            for j in range(2 * KB // 128):
                xf = xv[c, rows, j * 128 : j * 128 + 128].astype(F32)
                part = part + xf * xf
            sq[rows, :] = part
            return 0

        lax.fori_loop(0, ROWS // SQ_TILE, tile, 0)
        return 0

    lax.fori_loop(0, 4, squares, 0)
    w_c.wait()

    pl.semaphore_wait(barrier, NR - 1 + 3)

    def send_tag(d, _):
        p = (me + d) % NR
        rc(vtag, rtag.at[me], tag_ss.at[d], tag_rs.at[me], p).start()
        return 0

    lax.fori_loop(1, NR, send_tag, 0)
    w_all = Gather(lambda r: wv.at[r], lambda i: w_ss.at[i], lambda r: w_rs.at[r])
    w_all.first()

    def find_page(s, _):
        i = jnp.int32(0)
        for j in range(NP):
            i = jnp.where(slots[j] == s, j, i)
        page_of[s] = i
        return 0

    lax.fori_loop(0, 2 * NR, find_page, 0)

    acc[...] = jnp.zeros_like(acc)
    lax.fori_loop(4, 8, squares, 0)

    def invert(t, _):
        rows = pl.ds(pl.multiple_of(t * PAGE, PAGE), PAGE)
        mean = jnp.sum(sq[rows, :], axis=1, keepdims=True) * (1.0 / (NR * KB))
        sq[rows, :] = jnp.broadcast_to(lax.rsqrt(mean + EPSILON), (PAGE, 128))
        return 0

    lax.fori_loop(0, NP, invert, 0)

    dkv_c.wait()
    kv_c.wait()

    def attend(r, _):
        q = qb[r]
        pages = [kv[bt_ref[j, r]] for j in range(4)]
        own = dkv[...]
        keys = jnp.concatenate([p[:, :HS] for p in pages], axis=0)
        values = jnp.concatenate([p[:, HS:] for p in pages], axis=0)
        s1 = lax.dot_general(q, keys, NT_DIMS, preferred_element_type=F32) * SCALING
        s2 = lax.dot_general(q, own[:, :HS], NT_DIMS, preferred_element_type=F32) * SCALING
        col = lax.broadcasted_iota(jnp.int32, s1.shape, 1)
        s1 = jnp.where(col < len_ref[r], s1, LOW)
        col2 = lax.broadcasted_iota(jnp.int32, s2.shape, 1)
        row2 = lax.broadcasted_iota(jnp.int32, s2.shape, 0)
        s2 = jnp.where((col2 % RQ == r) & (col2 // RQ <= row2 // PER), s2, LOW)
        top = jnp.maximum(jnp.max(s1, axis=1, keepdims=True), jnp.max(s2, axis=1, keepdims=True))
        p1 = jnp.exp(s1 - top)
        p2 = jnp.exp(s2 - top)
        total = jnp.sum(p1, axis=1, keepdims=True) + jnp.sum(p2, axis=1, keepdims=True)
        o = jnp.dot(p1.astype(BF), values, preferred_element_type=F32)
        o = o + jnp.dot(p2.astype(BF), own[:, HS:], preferred_element_type=F32)
        ac[pl.ds(r, RQ, stride=RQ), :] = o / total
        lc[pl.ds(r, RQ, stride=RQ), :] = jnp.broadcast_to(top + jnp.log(total), (RQ, HS))
        return 0

    def ask():
        tmat = jnp.full((8, 128), -1, jnp.int32)

        def wait_tag(d, t):
            p = (me - d + NR) % NR

            @pl.when(d > 0)
            def _():
                rc(vtag, rtag.at[p], tag_ss.at[0], tag_rs.at[p], p).wait_recv()

            moved = pltpu.roll(rtag[p], (2 * p - 2 * me + 128) % 128, 1)
            return jnp.where(lane // 2 == p, moved, t)

        tmat = lax.fori_loop(0, NR, wait_tag, tmat)
        tvec[...] = tmat
        t_c = pltpu.make_async_copy(tvec, tsm, t_sem)
        t_c.start()
        t_c.wait()

        def pick(s, _):
            qs[s] = qb[jnp.maximum(tsm[0, s], 0)]
            return 0

        lax.fori_loop(0, 2 * NR, pick, 0, unroll=4)

        def send_q(d, _):
            p = (me + d) % NR
            rc(qs.at[pl.ds(2 * p, 2)], qr.at[pl.ds(2 * me, 2)], q_ss.at[d], q_rs.at[me], p).start()
            return 0

        lax.fori_loop(1, NR, send_q, 0)
        qr[pl.ds(2 * me, 2)] = qs[pl.ds(2 * me, 2)]

    def project(c):
        def tile(t, _):
            rows = pl.ds(pl.multiple_of(t * TILE, TILE), TILE)
            inverse = sq[rows, :]
            normed = []
            for j in range(2 * KB // 128):
                gain = gain_ref[2 * c + j // 4, j % 4 : j % 4 + 1, :].astype(F32)
                xf = xv[c, rows, j * 128 : j * 128 + 128].astype(F32)
                normed.append((xf * inverse * gain).astype(BF))
            normed = jnp.concatenate(normed, axis=1)
            acc[rows, :] += jnp.dot(normed, wv[pl.ds(2 * c, 2)].reshape(2 * KB, KVW), preferred_element_type=F32)
            return 0

        lax.fori_loop(0, ROWS // TILE, tile, 0)

    def group(i, _):
        lax.fori_loop(0, 8, lambda r, carry: attend(8 * i + r, carry), 0, unroll=UNROLL)

        @pl.when(i == 1)
        def _():
            ask()
            w_all.relay_near()

        @pl.when(i == 2)
        def _():
            w_all.wait(sib)
            project(chip)
            w_all.relay_far()

        return 0

    lax.fori_loop(0, RQ // 8, group, 0)

    def next_chip(i, _):
        c = chip_at(i % 4, i // 4)
        w_all.from_sib(c)
        project(c)
        return 0

    lax.fori_loop(1, 5, next_chip, 0)
    w_all.late()
    lax.fori_loop(5, 8, next_chip, 0)

    def wait_q(d, _):
        p = (me - d + NR) % NR
        rc(qs.at[pl.ds(0, 2)], qr.at[pl.ds(2 * p, 2)], q_ss.at[0], q_rs.at[p], p).wait_recv()
        return 0

    lax.fori_loop(1, NR, wait_q, 0)
    bias = bias_ref[...].astype(F32)
    bias = jnp.concatenate([bias[0:1], bias[1:2]], axis=1)
    lane_k = lax.broadcasted_iota(jnp.int32, (RQ, 128), 1)

    def page(i, st):
        rows = pl.ds(pl.multiple_of(i * PAGE, PAGE), PAGE)
        f = (acc[rows, :] + bias).astype(BF)
        slot = slot_of[i]
        q = qr[slot]
        s = lax.dot_general(q, f[:, :HS], NT_DIMS, preferred_element_type=F32) * SCALING
        top = jnp.max(s, axis=1, keepdims=True)
        p = jnp.exp(s - top)
        total = jnp.sum(p, axis=1, keepdims=True)
        o = jnp.dot(p.astype(BF), f[:, HS:], preferred_element_type=F32) / total
        pacc[i] = o.astype(BF)
        return jnp.where(lane_k == slot, top + jnp.log(total), st)

    st = lax.fori_loop(0, NP, page, jnp.full((RQ, 128), LOW, F32), unroll=True)
    packed = st[0:8]
    for a in range(1, 4):
        packed = jnp.where(lane // 32 == a, pltpu.roll(st[8 * a : 8 * a + 8], 32 * a, 1), packed)
    sst[...] = packed
    rst[me] = packed

    def place(s, _):
        accs[s] = pacc[page_of[s]]
        return 0

    lax.fori_loop(0, 2 * NR, place, 0, unroll=4)

    def send_acc(d, _):
        p = (me + d) % NR
        rc(accs.at[pl.ds(2 * p, 2)], racc.at[pl.ds(2 * me, 2)], a_ss.at[d], a_rs.at[me], p).start()
        rc(sst, rst.at[me], l_ss.at[d], l_rs.at[me], p).start()
        return 0

    lax.fori_loop(1, NR, send_acc, 0)
    racc[pl.ds(2 * me, 2)] = accs[pl.ds(2 * me, 2)]

    lt[...] = jnp.full((RQ, 128), LOW, F32)

    def wait_acc(d, _):
        p = (me - d + NR) % NR
        rc(sst, rst.at[p], l_ss.at[0], l_rs.at[p], p).wait_recv()
        rc(accs.at[pl.ds(0, 2)], racc.at[pl.ds(2 * p, 2)], a_ss.at[0], a_rs.at[p], p).wait_recv()
        return 0

    lax.fori_loop(1, NR, wait_acc, 0)

    def take(p, _):
        got = rst[p]
        for a in range(4):
            moved = pltpu.roll(got, (2 * p - 2 * me - 32 * a + 256) % 128, 1)
            lt[8 * a : 8 * a + 8, :] = jnp.where(lane // 2 == p, moved, lt[8 * a : 8 * a + 8, :])
        for c in range(2):
            sb[pl.ds(2 * p + c, RQ, stride=RQ), :] = racc[2 * p + c].astype(F32)
        return 0

    lax.fori_loop(0, NR, take, 0, unroll=4)

    mine = jnp.broadcast_to(tvec[0:1, :], (RQ, 128)) == lax.broadcasted_iota(jnp.int32, (RQ, 128), 0)

    def outputs(s):
        return Gather(lambda r: aall.at[s, r], lambda i: g_ss.at[s, i], lambda r: g_rs.at[s, r])

    def merge(s):
        for h in range(PER):
            k = s * PER + h
            rows = pl.ds(pl.multiple_of(k * RQ, RQ), RQ)
            scores = jnp.where(mine, jnp.broadcast_to(lt[pl.ds(k, 1), :], (RQ, 128)), LOW)
            base = lc[rows, :]
            top = jnp.maximum(jnp.max(scores, axis=1, keepdims=True), base)
            e = jnp.exp(scores - top)
            wc = jnp.exp(base - top)
            total = wc + jnp.sum(e, axis=1, keepdims=True)
            pv = jnp.dot(e[:, : 2 * NR].astype(BF), sb[rows, :].astype(BF), preferred_element_type=F32)
            merged = (wc * ac[rows, :] + pv) / total
            aall[s, me, :, h * HS : (h + 1) * HS] = merged.astype(BF)
        outputs(s).first()

    x_p, x_m, x_2 = (xx + 1) % 4, (xx + 3) % 4, (xx + 2) % 4

    def x_send(s, i):
        to = x_m if i % 2 else x_p
        src, dst = (
            (ps.at[s, x_2, 0], pa.at[s, 0]),
            (ps.at[s, x_2, 1], pa.at[s, 1]),
            (ps.at[s, x_p, 1], px.at[s, 0, 1]),
            (ps.at[s, x_m, 0], px.at[s, 1, 0]),
            (ps.at[s, x_p, 0], px.at[s, 0, 0]),
            (ps.at[s, x_m, 1], px.at[s, 1, 1]),
        )[i]
        return rc(src, dst, p_ss.at[s, i], p_rs.at[s, i], me, 4 * yl + to)

    def relay_x(s):
        x_send(s, 0).wait_recv()
        ps[s, x_p, 0] = (ps[s, x_p, 0].astype(F32) + pa[s, 0].astype(F32)).astype(BF)
        x_send(s, 4).start()
        x_send(s, 1).wait_recv()
        ps[s, x_m, 1] = (ps[s, x_m, 1].astype(F32) + pa[s, 1].astype(F32)).astype(BF)
        x_send(s, 5).start()

    def y_send(s):
        return rc(ys.at[s], py.at[s], y_ss.at[s], y_rs.at[s], me, 4 * (1 - yl) + xx)

    def product(s):
        g = outputs(s)
        g.late()
        g.wait(sib)
        for c in chips[1:]:
            g.from_sib(c)

        def part(j, _):
            a = aall[s, pl.ds(j * 8, 8)].reshape(8 * RQ, 1024)
            o = jnp.dot(a, wout[...], preferred_element_type=F32).astype(BF)
            o = o.reshape(4, 2 * RQ, NOUT)
            for i in range(4):
                for h in range(2):
                    ps[s, i, h, j] = o[i, :, h * 256 : h * 256 + 256]
            return 0

        lax.fori_loop(0, 2, part, 0)
        for i in range(4):
            x_send(s, i).start()

    def add_x(s):
        for i in range(2, 6):
            x_send(s, i).wait_recv()
        for half in range(2):
            o = jnp.concatenate(
                [
                    ps[s, xx, h, half].astype(F32) + px[s, 0, h, half].astype(F32) + px[s, 1, h, half].astype(F32)
                    for h in range(2)
                ],
                axis=1,
            )

            @pl.when(yl == half)
            def _():
                ko[s] = o

            @pl.when(yl != half)
            def _():
                ys[s] = o.astype(BF)

        y_send(s).start()

    def add_y(s):
        y_send(s).wait_recv()
        out_ref[s] = (ko[s] + py[s].astype(F32)).astype(BF)

    merge(0)
    merge(1)
    wout_c.wait()

    def round_(i, _):
        @pl.when(i < STEPS)
        def _():
            outputs(i).relay_near()
            outputs(i).relay_far()

        @pl.when(i < STEPS - 2)
        def _():
            merge(i + 2)

        @pl.when((i >= 1) & (i <= STEPS))
        def _():
            product(i - 1)

        @pl.when((i >= 2) & (i <= STEPS + 1))
        def _():
            relay_x(i - 2)

        @pl.when((i >= 3) & (i <= STEPS + 2))
        def _():
            add_x(i - 3)

        @pl.when(i >= 4)
        def _():
            add_y(i - 4)

        return 0

    lax.fori_loop(0, STEPS + 4, round_, 0)

    def drain(d, _):
        rc(vtag, rtag.at[me], tag_ss.at[d], tag_rs.at[me], sib).wait_send()
        rc(qs.at[pl.ds(0, 2)], qr.at[pl.ds(0, 2)], q_ss.at[d], q_rs.at[me], sib).wait_send()
        rc(accs.at[pl.ds(0, 2)], racc.at[pl.ds(0, 2)], a_ss.at[d], a_rs.at[me], sib).wait_send()
        rc(sst, rst.at[me], l_ss.at[d], l_rs.at[me], sib).wait_send()
        return 0

    lax.fori_loop(1, NR, drain, 0)
    w_all.drain()

    def drain_s(s, _):
        outputs(s).drain()
        for i in range(6):
            x_send(s, i).wait_send()
        y_send(s).wait_send()
        return 0

    lax.fori_loop(0, STEPS, drain_s, 0)


def body(
    x_pre,
    ln_gain,
    w_kv,
    kv_bias,
    page_owner,
    page_req,
    kv_pool,
    block_table,
    cache_len,
    dec_q,
    dec_kv,
    w_out,
):
    any_spec = pl.BlockSpec(memory_space=pl.ANY)
    smem = pl.BlockSpec(memory_space=pltpu.SMEM)
    vmem = pl.BlockSpec(memory_space=pltpu.VMEM)
    dma = pltpu.SemaphoreType.DMA
    V = pltpu.VMEM
    scratch = [
        V((8, ROWS, 2 * KB), BF),
        V((NR, KB, KVW), BF),
        V((32, PAGE, KVW), BF),
        V((STEPS, RQ, 1024), BF),
        V((STEPS * RQ, KVW), BF),
        V((1024, NOUT), BF),
        V((ROWS, KVW), F32),
        V((ROWS, 128), F32),
        V((RQ * RQ, HS), F32),
        V((RQ, RQ, HS), BF),
        V((RQ * RQ, HS), F32),
        V((RQ * RQ, HS), F32),
        V((8, 128), jnp.int32),
        V((NR, 8, 128), jnp.int32),
        V((8, 128), jnp.int32),
        pltpu.SMEM((8, 128), jnp.int32),
        pltpu.SMEM((16,), jnp.int32),
        pltpu.SMEM((2 * NR,), jnp.int32),
        V((2 * NR, RQ, HS), BF),
        V((2 * NR, RQ, HS), BF),
        V((NP, RQ, HS), BF),
        V((2 * NR, RQ, HS), BF),
        V((2 * NR, RQ, HS), BF),
        V((8, 128), F32),
        V((NR, 8, 128), F32),
        V((RQ, 128), F32),
        V((RQ * RQ, HS), F32),
        V((STEPS, NR, RQ, 1024), BF),
        V((STEPS, 4, 2, 2, 2 * RQ, 256), BF),
        V((STEPS, 2, 2, 2 * RQ, 256), BF),
        V((STEPS, 2, 2, 2, 2 * RQ, 256), BF),
        V((STEPS, 2 * RQ, NOUT), BF),
        V((STEPS, 2 * RQ, NOUT), BF),
        V((STEPS, 2 * RQ, NOUT), F32),
        dma((8,)),
        dma((5,)),
        dma,
        dma((15,)),
        dma((NR,)),
        dma((NR,)),
        dma((NR,)),
        dma((NR,)),
        dma((NR,)),
        dma((NR,)),
        dma((NR,)),
        dma((NR,)),
        dma((NR,)),
        dma((STEPS, 15)),
        dma((STEPS, NR)),
        dma((STEPS, 6)),
        dma((STEPS, 6)),
        dma((STEPS,)),
        dma((STEPS,)),
    ]
    return pl.pallas_call(
        kernel,
        out_shape=jax.ShapeDtypeStruct((STEPS, 2 * RQ, NOUT), BF),
        in_specs=[any_spec, vmem, any_spec, vmem, smem, smem, any_spec, smem, smem, any_spec, any_spec, any_spec],
        out_specs=vmem,
        scratch_shapes=scratch,
        compiler_params=pltpu.CompilerParams(
            collective_id=0, has_side_effects=True, vmem_limit_bytes=58 * 1024 * 1024
        ),
    )(
        x_pre,
        ln_gain.reshape(NR, KB // 128, 128),
        w_kv,
        kv_bias.reshape(2, HS),
        page_owner.T,
        page_req,
        kv_pool,
        block_table.T,
        cache_len,
        dec_q,
        dec_kv.reshape(STEPS * RQ, KVW),
        w_out,
    )


def solution(mesh):
    return jax.shard_map(
        body,
        mesh=mesh,
        in_specs=(
            P("role", None),
            P(),
            P("role", "tp"),
            P("tp"),
            P("role", None),
            P("role"),
            P("role", None, "tp"),
            P("role", None),
            P("role"),
            P(None, "role", "tp"),
            P(None, "role", "tp"),
            P("tp", "role"),
        ),
        out_specs=P(None, "tp", "role"),
        check_vma=False,
    )
```

```python
import functools
import math

import jax
import jax.numpy as jnp
from jax import lax
from jax.experimental import pallas as pl
from jax.experimental.pallas import tpu as pltpu
from jax.sharding import PartitionSpec as P

HS = 128
PAGE = 128
EPSILON = 1e-06
LOW = -1e30
MESH = pl.DeviceIdType.MESH
BF = jnp.bfloat16
F32 = jnp.float32

NR = 16
NT = 8
NP = 11
RQ = 32
STEPS = 4
PER = 8
KB = 512
KVW = 256
ROWS = NP * PAGE
TILE = 704
SQ_TILE = 176
UNROLL = 4
NOUT = 512
SCALING = 1.0 / math.sqrt(HS)
NT_DIMS = (((1,), (1,)), ((), ()))


def kernel(
    x_hbm,
    gain_ref,
    w_hbm,
    bias_ref,
    owner_ref,
    req_ref,
    kv_hbm,
    bt_ref,
    len_ref,
    dq_hbm,
    dkv_hbm,
    wout_hbm,
    out_ref,
    xv,
    wv,
    kv,
    dq,
    dkv,
    wout,
    acc,
    sq,
    qf,
    qb,
    ac,
    lc,
    vtag,
    rtag,
    tvec,
    tsm,
    slot_of,
    page_of,
    qs,
    qr,
    pacc,
    accs,
    racc,
    sst,
    rst,
    lt,
    sb,
    aall,
    ps,
    pa,
    px,
    ys,
    py,
    ko,
    x_sem,
    in_sem,
    t_sem,
    w_ss,
    w_rs,
    tag_ss,
    tag_rs,
    q_ss,
    q_rs,
    a_ss,
    a_rs,
    l_ss,
    l_rs,
    g_ss,
    g_rs,
    p_ss,
    p_rs,
    y_ss,
    y_rs,
):
    me = lax.axis_index("role")
    tp = lax.axis_index("tp")
    chip, core = me // 2, me % 2
    z, yh = chip // 2, chip % 2
    yl, xx = tp // 4, tp % 4
    sib = 2 * chip + (1 - core)

    def chip_at(dz, dy):
        return ((z + dz) % 4) * 2 + (yh + dy) % 2

    c_y, c_p, c_m, c_2 = chip_at(0, 1), chip_at(1, 0), chip_at(3, 0), chip_at(2, 0)
    c_yp, c_ym, c_y2 = chip_at(1, 1), chip_at(3, 1), chip_at(2, 1)

    def rc(src, dst, ss, rs, role, t=None):
        return pltpu.make_async_remote_copy(
            src_ref=src,
            dst_ref=dst,
            send_sem=ss,
            recv_sem=rs,
            device_id=(role, tp if t is None else t),
            device_id_type=MESH,
        )

    class Gather:
        def __init__(self, block, ss, rs):
            self.block, self.ss, self.rs = block, ss, rs

        def copy(self, i, of, to):
            return rc(self.block(of), self.block(of), self.ss(i), self.rs(of), to)

        def ops(self):
            ch = lambda c: 2 * c + core
            return [
                (me, ch(c_y)),
                (me, ch(c_p)),
                (me, ch(c_m)),
                (me, ch(c_2)),
                (me, sib),
                (ch(c_y), ch(c_p)),
                (ch(c_y), ch(c_m)),
                (ch(c_2), ch(c_y)),
            ] + [(ch(c), sib) for c in (c_p, c_m, c_y, c_2, c_yp, c_ym, c_y2)]

        def start(self, *which):
            ops = self.ops()
            for i in which:
                self.copy(i, *ops[i]).start()

        def wait(self, role):
            self.copy(0, role, sib).wait_recv()

        def first(self):
            self.start(0, 1, 2, 3, 4)

        def relay_near(self):
            self.wait(2 * c_y + core)
            self.start(5, 6, 10)
            self.wait(2 * c_p + core)
            self.start(8)
            self.wait(2 * c_m + core)
            self.start(9)

        def relay_far(self):
            self.wait(2 * c_2 + core)
            self.start(7, 11)

        def late(self):
            for i, c in ((12, c_yp), (13, c_ym), (14, c_y2)):
                self.wait(2 * c + core)
                self.start(i)

        def from_sib(self, c):
            self.wait(2 * c + (1 - core))

        def drain(self):
            ops = self.ops()
            for i in range(15):
                self.copy(i, *ops[i]).wait_send()

    def x_copy(c):
        return pltpu.make_async_copy(
            x_hbm.at[:, pl.ds(pl.multiple_of(c * 2 * KB, 2 * KB), 2 * KB)], xv.at[c], x_sem.at[c]
        )

    w_c = pltpu.make_async_copy(w_hbm, wv.at[me], in_sem.at[0])
    kv_c = pltpu.make_async_copy(kv_hbm, kv, in_sem.at[1])
    dq_c = pltpu.make_async_copy(dq_hbm, dq, in_sem.at[2])
    dkv_c = pltpu.make_async_copy(dkv_hbm, dkv, in_sem.at[3])
    wout_c = pltpu.make_async_copy(wout_hbm, wout, in_sem.at[4])
    w_c.start()
    dq_c.start()
    dkv_c.start()
    kv_c.start()

    barrier = pltpu.get_barrier_semaphore()

    def greet_role(d, _):
        pl.semaphore_signal(barrier, inc=1, device_id=((me + d) % NR, tp), device_id_type=MESH)
        return 0

    lax.fori_loop(1, NR, greet_role, 0)
    for d in (1, 3):
        pl.semaphore_signal(barrier, inc=1, device_id=(me, 4 * yl + (xx + d) % 4), device_id_type=MESH)
    pl.semaphore_signal(barrier, inc=1, device_id=(me, 4 * (1 - yl) + xx), device_id_type=MESH)

    chips = [chip_at(i % 4, i // 4) for i in range(8)]
    for c in chips:
        x_copy(c).start()
    wout_c.start()

    lane = lax.broadcasted_iota(jnp.int32, (8, 128), 1)
    owners = [owner_ref[0, i] for i in range(NP)]
    tags = jnp.full((8, 128), -1, jnp.int32)
    slots = []
    for i in range(NP):
        rank = jnp.int32(0)
        for j in range(i):
            rank = rank + (owners[j] == owners[i]).astype(jnp.int32)
        slot = 2 * owners[i] + rank
        slots.append(slot)
        slot_of[i] = slot
        tags = jnp.where(lane == slot, req_ref[i], tags)
    vtag[...] = tags
    rtag[me] = tags

    sq[...] = jnp.zeros_like(sq)

    def squares(i, _):
        c = chip_at(i % 4, i // 4)
        x_copy(c).wait()

        def tile(t, _):
            rows = pl.ds(pl.multiple_of(t * SQ_TILE, SQ_TILE), SQ_TILE)
            part = sq[rows, :]
            for j in range(2 * KB // 128):
                xf = xv[c, rows, j * 128 : j * 128 + 128].astype(F32)
                part = part + xf * xf
            sq[rows, :] = part
            return 0

        lax.fori_loop(0, ROWS // SQ_TILE, tile, 0)
        return 0

    w_c.wait()

    pl.semaphore_wait(barrier, NR - 1 + 3)

    def send_tag(d, _):
        p = (me + d) % NR
        rc(vtag, rtag.at[me], tag_ss.at[d], tag_rs.at[me], p).start()
        return 0

    lax.fori_loop(1, NR, send_tag, 0)
    w_all = Gather(lambda r: wv.at[r], lambda i: w_ss.at[i], lambda r: w_rs.at[r])
    w_all.first()

    dq_c.wait()
    for s in range(STEPS):
        for h in range(PER):
            qf[pl.ds(s * PER + h, RQ, stride=RQ), :] = dq[s, :, h * HS : (h + 1) * HS].astype(F32)

    def by_request(r, _):
        qb[r] = qf[pl.ds(pl.multiple_of(r * RQ, RQ), RQ), :].astype(BF)
        return 0

    lax.fori_loop(0, RQ, by_request, 0, unroll=4)

    def find_page(s, _):
        i = jnp.int32(0)
        for j in range(NP):
            i = jnp.where(slots[j] == s, j, i)
        page_of[s] = i
        return 0

    lax.fori_loop(0, 2 * NR, find_page, 0)

    acc[...] = jnp.zeros_like(acc)
    lax.fori_loop(0, 8, squares, 0)

    def invert(t, _):
        rows = pl.ds(pl.multiple_of(t * PAGE, PAGE), PAGE)
        mean = jnp.sum(sq[rows, :], axis=1, keepdims=True) * (1.0 / (NR * KB))
        sq[rows, :] = jnp.broadcast_to(lax.rsqrt(mean + EPSILON), (PAGE, 128))
        return 0

    lax.fori_loop(0, NP, invert, 0)

    dkv_c.wait()
    kv_c.wait()

    def attend(r, _):
        q = qb[r]
        pages = [kv[bt_ref[j, r]] for j in range(4)]
        own = dkv[...]
        keys = jnp.concatenate([p[:, :HS] for p in pages], axis=0)
        values = jnp.concatenate([p[:, HS:] for p in pages], axis=0)
        s1 = lax.dot_general(q, keys, NT_DIMS, preferred_element_type=F32) * SCALING
        s2 = lax.dot_general(q, own[:, :HS], NT_DIMS, preferred_element_type=F32) * SCALING
        col = lax.broadcasted_iota(jnp.int32, s1.shape, 1)
        s1 = jnp.where(col < len_ref[r], s1, LOW)
        col2 = lax.broadcasted_iota(jnp.int32, s2.shape, 1)
        row2 = lax.broadcasted_iota(jnp.int32, s2.shape, 0)
        s2 = jnp.where((col2 % RQ == r) & (col2 // RQ <= row2 // PER), s2, LOW)
        top = jnp.maximum(jnp.max(s1, axis=1, keepdims=True), jnp.max(s2, axis=1, keepdims=True))
        p1 = jnp.exp(s1 - top)
        p2 = jnp.exp(s2 - top)
        total = jnp.sum(p1, axis=1, keepdims=True) + jnp.sum(p2, axis=1, keepdims=True)
        o = jnp.dot(p1.astype(BF), values, preferred_element_type=F32)
        o = o + jnp.dot(p2.astype(BF), own[:, HS:], preferred_element_type=F32)
        ac[pl.ds(r, RQ, stride=RQ), :] = o / total
        lc[pl.ds(r, RQ, stride=RQ), :] = jnp.broadcast_to(top + jnp.log(total), (RQ, HS))
        return 0

    def ask():
        tmat = jnp.full((8, 128), -1, jnp.int32)

        def wait_tag(d, t):
            p = (me - d + NR) % NR

            @pl.when(d > 0)
            def _():
                rc(vtag, rtag.at[p], tag_ss.at[0], tag_rs.at[p], p).wait_recv()

            moved = pltpu.roll(rtag[p], (2 * p - 2 * me + 128) % 128, 1)
            return jnp.where(lane // 2 == p, moved, t)

        tmat = lax.fori_loop(0, NR, wait_tag, tmat)
        tvec[...] = tmat
        t_c = pltpu.make_async_copy(tvec, tsm, t_sem)
        t_c.start()
        t_c.wait()

        def pick(s, _):
            qs[s] = qb[jnp.maximum(tsm[0, s], 0)]
            return 0

        lax.fori_loop(0, 2 * NR, pick, 0, unroll=4)

        def send_q(d, _):
            p = (me + d) % NR
            rc(qs.at[pl.ds(2 * p, 2)], qr.at[pl.ds(2 * me, 2)], q_ss.at[d], q_rs.at[me], p).start()
            return 0

        lax.fori_loop(1, NR, send_q, 0)
        qr[pl.ds(2 * me, 2)] = qs[pl.ds(2 * me, 2)]

    def project(c):
        def tile(t, _):
            rows = pl.ds(pl.multiple_of(t * TILE, TILE), TILE)
            inverse = sq[rows, :]
            normed = []
            for j in range(2 * KB // 128):
                gain = gain_ref[2 * c + j // 4, j % 4 : j % 4 + 1, :].astype(F32)
                xf = xv[c, rows, j * 128 : j * 128 + 128].astype(F32)
                normed.append((xf * inverse * gain).astype(BF))
            normed = jnp.concatenate(normed, axis=1)
            acc[rows, :] += jnp.dot(normed, wv[pl.ds(2 * c, 2)].reshape(2 * KB, KVW), preferred_element_type=F32)
            return 0

        lax.fori_loop(0, ROWS // TILE, tile, 0)

    def group(i, _):
        lax.fori_loop(0, 8, lambda r, carry: attend(8 * i + r, carry), 0, unroll=UNROLL)

        @pl.when(i == 1)
        def _():
            ask()
            w_all.relay_near()

        @pl.when(i == 2)
        def _():
            w_all.wait(sib)
            project(chip)
            w_all.relay_far()

        return 0

    lax.fori_loop(0, RQ // 8, group, 0)

    def next_chip(i, _):
        c = chip_at(i % 4, i // 4)
        w_all.from_sib(c)
        project(c)
        return 0

    lax.fori_loop(1, 5, next_chip, 0)
    w_all.late()
    lax.fori_loop(5, 8, next_chip, 0)

    def wait_q(d, _):
        p = (me - d + NR) % NR
        rc(qs.at[pl.ds(0, 2)], qr.at[pl.ds(2 * p, 2)], q_ss.at[0], q_rs.at[p], p).wait_recv()
        return 0

    lax.fori_loop(1, NR, wait_q, 0)
    bias = bias_ref[...].astype(F32)
    bias = jnp.concatenate([bias[0:1], bias[1:2]], axis=1)
    lane_k = lax.broadcasted_iota(jnp.int32, (RQ, 128), 1)

    def page(i, st):
        rows = pl.ds(pl.multiple_of(i * PAGE, PAGE), PAGE)
        f = (acc[rows, :] + bias).astype(BF)
        slot = slot_of[i]
        q = qr[slot]
        s = lax.dot_general(q, f[:, :HS], NT_DIMS, preferred_element_type=F32) * SCALING
        top = jnp.max(s, axis=1, keepdims=True)
        p = jnp.exp(s - top)
        total = jnp.sum(p, axis=1, keepdims=True)
        o = jnp.dot(p.astype(BF), f[:, HS:], preferred_element_type=F32) / total
        pacc[i] = o.astype(BF)
        return jnp.where(lane_k == slot, top + jnp.log(total), st)

    st = lax.fori_loop(0, NP, page, jnp.full((RQ, 128), LOW, F32), unroll=True)
    packed = st[0:8]
    for a in range(1, 4):
        packed = jnp.where(lane // 32 == a, pltpu.roll(st[8 * a : 8 * a + 8], 32 * a, 1), packed)
    sst[...] = packed
    rst[me] = packed

    def place(s, _):
        accs[s] = pacc[page_of[s]]
        return 0

    lax.fori_loop(0, 2 * NR, place, 0, unroll=4)

    def send_acc(d, _):
        p = (me + d) % NR
        rc(accs.at[pl.ds(2 * p, 2)], racc.at[pl.ds(2 * me, 2)], a_ss.at[d], a_rs.at[me], p).start()
        rc(sst, rst.at[me], l_ss.at[d], l_rs.at[me], p).start()
        return 0

    lax.fori_loop(1, NR, send_acc, 0)
    racc[pl.ds(2 * me, 2)] = accs[pl.ds(2 * me, 2)]

    lt[...] = jnp.full((RQ, 128), LOW, F32)

    def wait_acc(d, _):
        p = (me - d + NR) % NR
        rc(sst, rst.at[p], l_ss.at[0], l_rs.at[p], p).wait_recv()
        rc(accs.at[pl.ds(0, 2)], racc.at[pl.ds(2 * p, 2)], a_ss.at[0], a_rs.at[p], p).wait_recv()
        return 0

    lax.fori_loop(1, NR, wait_acc, 0)

    def take(p, _):
        got = rst[p]
        for a in range(4):
            moved = pltpu.roll(got, (2 * p - 2 * me - 32 * a + 256) % 128, 1)
            lt[8 * a : 8 * a + 8, :] = jnp.where(lane // 2 == p, moved, lt[8 * a : 8 * a + 8, :])
        for c in range(2):
            sb[pl.ds(2 * p + c, RQ, stride=RQ), :] = racc[2 * p + c].astype(F32)
        return 0

    lax.fori_loop(0, NR, take, 0, unroll=4)

    mine = jnp.broadcast_to(tvec[0:1, :], (RQ, 128)) == lax.broadcasted_iota(jnp.int32, (RQ, 128), 0)

    def outputs(s):
        return Gather(lambda r: aall.at[s, r], lambda i: g_ss.at[s, i], lambda r: g_rs.at[s, r])

    def merge(s):
        for h in range(PER):
            k = s * PER + h
            rows = pl.ds(pl.multiple_of(k * RQ, RQ), RQ)
            scores = jnp.where(mine, jnp.broadcast_to(lt[pl.ds(k, 1), :], (RQ, 128)), LOW)
            base = lc[rows, :]
            top = jnp.maximum(jnp.max(scores, axis=1, keepdims=True), base)
            e = jnp.exp(scores - top)
            wc = jnp.exp(base - top)
            total = wc + jnp.sum(e, axis=1, keepdims=True)
            pv = jnp.dot(e[:, : 2 * NR].astype(BF), sb[rows, :].astype(BF), preferred_element_type=F32)
            merged = (wc * ac[rows, :] + pv) / total
            aall[s, me, :, h * HS : (h + 1) * HS] = merged.astype(BF)
        outputs(s).first()

    x_p, x_m, x_2 = (xx + 1) % 4, (xx + 3) % 4, (xx + 2) % 4

    def x_send(s, i):
        to = x_m if i % 2 else x_p
        src, dst = (
            (ps.at[s, x_2, 0], pa.at[s, 0]),
            (ps.at[s, x_2, 1], pa.at[s, 1]),
            (ps.at[s, x_p, 1], px.at[s, 0, 1]),
            (ps.at[s, x_m, 0], px.at[s, 1, 0]),
            (ps.at[s, x_p, 0], px.at[s, 0, 0]),
            (ps.at[s, x_m, 1], px.at[s, 1, 1]),
        )[i]
        return rc(src, dst, p_ss.at[s, i], p_rs.at[s, i], me, 4 * yl + to)

    def relay_x(s):
        x_send(s, 0).wait_recv()
        ps[s, x_p, 0] = (ps[s, x_p, 0].astype(F32) + pa[s, 0].astype(F32)).astype(BF)
        x_send(s, 4).start()
        x_send(s, 1).wait_recv()
        ps[s, x_m, 1] = (ps[s, x_m, 1].astype(F32) + pa[s, 1].astype(F32)).astype(BF)
        x_send(s, 5).start()

    def y_send(s):
        return rc(ys.at[s], py.at[s], y_ss.at[s], y_rs.at[s], me, 4 * (1 - yl) + xx)

    def product(s):
        g = outputs(s)
        g.late()
        g.wait(sib)
        for c in chips[1:]:
            g.from_sib(c)

        def part(j, _):
            a = aall[s, pl.ds(j * 8, 8)].reshape(8 * RQ, 1024)
            o = jnp.dot(a, wout[...], preferred_element_type=F32).astype(BF)
            o = o.reshape(4, 2 * RQ, NOUT)
            for i in range(4):
                for h in range(2):
                    ps[s, i, h, j] = o[i, :, h * 256 : h * 256 + 256]
            return 0

        lax.fori_loop(0, 2, part, 0)
        for i in range(4):
            x_send(s, i).start()

    def add_x(s):
        for i in range(2, 6):
            x_send(s, i).wait_recv()
        for half in range(2):
            o = jnp.concatenate(
                [
                    ps[s, xx, h, half].astype(F32) + px[s, 0, h, half].astype(F32) + px[s, 1, h, half].astype(F32)
                    for h in range(2)
                ],
                axis=1,
            )

            @pl.when(yl == half)
            def _():
                ko[s] = o

            @pl.when(yl != half)
            def _():
                ys[s] = o.astype(BF)

        y_send(s).start()

    def add_y(s):
        y_send(s).wait_recv()
        out_ref[s] = (ko[s] + py[s].astype(F32)).astype(BF)

    merge(0)
    merge(1)
    wout_c.wait()

    def round_(i, _):
        @pl.when(i < STEPS)
        def _():
            outputs(i).relay_near()
            outputs(i).relay_far()

        @pl.when(i < STEPS - 2)
        def _():
            merge(i + 2)

        @pl.when((i >= 1) & (i <= STEPS))
        def _():
            product(i - 1)

        @pl.when((i >= 2) & (i <= STEPS + 1))
        def _():
            relay_x(i - 2)

        @pl.when((i >= 3) & (i <= STEPS + 2))
        def _():
            add_x(i - 3)

        @pl.when(i >= 4)
        def _():
            add_y(i - 4)

        return 0

    lax.fori_loop(0, STEPS + 4, round_, 0)

    def drain(d, _):
        rc(vtag, rtag.at[me], tag_ss.at[d], tag_rs.at[me], sib).wait_send()
        rc(qs.at[pl.ds(0, 2)], qr.at[pl.ds(0, 2)], q_ss.at[d], q_rs.at[me], sib).wait_send()
        rc(accs.at[pl.ds(0, 2)], racc.at[pl.ds(0, 2)], a_ss.at[d], a_rs.at[me], sib).wait_send()
        rc(sst, rst.at[me], l_ss.at[d], l_rs.at[me], sib).wait_send()
        return 0

    lax.fori_loop(1, NR, drain, 0)
    w_all.drain()

    def drain_s(s, _):
        outputs(s).drain()
        for i in range(6):
            x_send(s, i).wait_send()
        y_send(s).wait_send()
        return 0

    lax.fori_loop(0, STEPS, drain_s, 0)


def body(
    x_pre,
    ln_gain,
    w_kv,
    kv_bias,
    page_owner,
    page_req,
    kv_pool,
    block_table,
    cache_len,
    dec_q,
    dec_kv,
    w_out,
):
    any_spec = pl.BlockSpec(memory_space=pl.ANY)
    smem = pl.BlockSpec(memory_space=pltpu.SMEM)
    vmem = pl.BlockSpec(memory_space=pltpu.VMEM)
    dma = pltpu.SemaphoreType.DMA
    V = pltpu.VMEM
    scratch = [
        V((8, ROWS, 2 * KB), BF),
        V((NR, KB, KVW), BF),
        V((32, PAGE, KVW), BF),
        V((STEPS, RQ, 1024), BF),
        V((STEPS * RQ, KVW), BF),
        V((1024, NOUT), BF),
        V((ROWS, KVW), F32),
        V((ROWS, 128), F32),
        V((RQ * RQ, HS), F32),
        V((RQ, RQ, HS), BF),
        V((RQ * RQ, HS), F32),
        V((RQ * RQ, HS), F32),
        V((8, 128), jnp.int32),
        V((NR, 8, 128), jnp.int32),
        V((8, 128), jnp.int32),
        pltpu.SMEM((8, 128), jnp.int32),
        pltpu.SMEM((16,), jnp.int32),
        pltpu.SMEM((2 * NR,), jnp.int32),
        V((2 * NR, RQ, HS), BF),
        V((2 * NR, RQ, HS), BF),
        V((NP, RQ, HS), BF),
        V((2 * NR, RQ, HS), BF),
        V((2 * NR, RQ, HS), BF),
        V((8, 128), F32),
        V((NR, 8, 128), F32),
        V((RQ, 128), F32),
        V((RQ * RQ, HS), F32),
        V((STEPS, NR, RQ, 1024), BF),
        V((STEPS, 4, 2, 2, 2 * RQ, 256), BF),
        V((STEPS, 2, 2, 2 * RQ, 256), BF),
        V((STEPS, 2, 2, 2, 2 * RQ, 256), BF),
        V((STEPS, 2 * RQ, NOUT), BF),
        V((STEPS, 2 * RQ, NOUT), BF),
        V((STEPS, 2 * RQ, NOUT), F32),
        dma((8,)),
        dma((5,)),
        dma,
        dma((15,)),
        dma((NR,)),
        dma((NR,)),
        dma((NR,)),
        dma((NR,)),
        dma((NR,)),
        dma((NR,)),
        dma((NR,)),
        dma((NR,)),
        dma((NR,)),
        dma((STEPS, 15)),
        dma((STEPS, NR)),
        dma((STEPS, 6)),
        dma((STEPS, 6)),
        dma((STEPS,)),
        dma((STEPS,)),
    ]
    return pl.pallas_call(
        kernel,
        out_shape=jax.ShapeDtypeStruct((STEPS, 2 * RQ, NOUT), BF),
        in_specs=[any_spec, vmem, any_spec, vmem, smem, smem, any_spec, smem, smem, any_spec, any_spec, any_spec],
        out_specs=vmem,
        scratch_shapes=scratch,
        compiler_params=pltpu.CompilerParams(
            collective_id=0, has_side_effects=True, vmem_limit_bytes=58 * 1024 * 1024
        ),
    )(
        x_pre,
        ln_gain.reshape(NR, KB // 128, 128),
        w_kv,
        kv_bias.reshape(2, HS),
        page_owner.T,
        page_req,
        kv_pool,
        block_table.T,
        cache_len,
        dec_q,
        dec_kv.reshape(STEPS * RQ, KVW),
        w_out,
    )


def solution(mesh):
    return jax.shard_map(
        body,
        mesh=mesh,
        in_specs=(
            P("role", None),
            P(),
            P("role", "tp"),
            P("tp"),
            P("role", None),
            P("role"),
            P("role", None, "tp"),
            P("role", None),
            P("role"),
            P(None, "role", "tp"),
            P(None, "role", "tp"),
            P("tp", "role"),
        ),
        out_specs=P(None, "tp", "role"),
        check_vma=False,
    )
```

```python
import functools
import math

import jax
import jax.numpy as jnp
from jax import lax
from jax.experimental import pallas as pl
from jax.experimental.pallas import tpu as pltpu
from jax.sharding import PartitionSpec as P

HS = 128
PAGE = 128
EPSILON = 1e-06
LOW = -1e30
MESH = pl.DeviceIdType.MESH
BF = jnp.bfloat16
F32 = jnp.float32

NR = 16
NT = 8
NP = 11
RQ = 32
STEPS = 4
PER = 8
KB = 512
KVW = 256
ROWS = NP * PAGE
TILE = 704
SQ_TILE = 352
UNROLL = 4
NOUT = 512
SCALING = 1.0 / math.sqrt(HS)
NT_DIMS = (((1,), (1,)), ((), ()))


def kernel(
    x_hbm,
    gain_ref,
    w_hbm,
    bias_ref,
    owner_ref,
    req_ref,
    kv_hbm,
    bt_ref,
    len_ref,
    dq_hbm,
    dkv_hbm,
    wout_hbm,
    out_ref,
    xv,
    wv,
    kv,
    dq,
    dkv,
    wout,
    acc,
    sq,
    qf,
    qb,
    ac,
    lc,
    vtag,
    rtag,
    tvec,
    tsm,
    slot_of,
    page_of,
    qs,
    qr,
    pacc,
    accs,
    racc,
    sst,
    rst,
    lt,
    sb,
    aall,
    ps,
    pa,
    px,
    ys,
    py,
    ko,
    x_sem,
    in_sem,
    t_sem,
    w_ss,
    w_rs,
    tag_ss,
    tag_rs,
    q_ss,
    q_rs,
    a_ss,
    a_rs,
    l_ss,
    l_rs,
    g_ss,
    g_rs,
    p_ss,
    p_rs,
    y_ss,
    y_rs,
):
    me = lax.axis_index("role")
    tp = lax.axis_index("tp")
    chip, core = me // 2, me % 2
    z, yh = chip // 2, chip % 2
    yl, xx = tp // 4, tp % 4
    sib = 2 * chip + (1 - core)

    def chip_at(dz, dy):
        return ((z + dz) % 4) * 2 + (yh + dy) % 2

    c_y, c_p, c_m, c_2 = chip_at(0, 1), chip_at(1, 0), chip_at(3, 0), chip_at(2, 0)
    c_yp, c_ym, c_y2 = chip_at(1, 1), chip_at(3, 1), chip_at(2, 1)

    def rc(src, dst, ss, rs, role, t=None):
        return pltpu.make_async_remote_copy(
            src_ref=src,
            dst_ref=dst,
            send_sem=ss,
            recv_sem=rs,
            device_id=(role, tp if t is None else t),
            device_id_type=MESH,
        )

    class Gather:
        def __init__(self, block, ss, rs):
            self.block, self.ss, self.rs = block, ss, rs

        def copy(self, i, of, to):
            return rc(self.block(of), self.block(of), self.ss(i), self.rs(of), to)

        def ops(self):
            ch = lambda c: 2 * c + core
            return [
                (me, ch(c_y)),
                (me, ch(c_p)),
                (me, ch(c_m)),
                (me, ch(c_2)),
                (me, sib),
                (ch(c_y), ch(c_p)),
                (ch(c_y), ch(c_m)),
                (ch(c_2), ch(c_y)),
            ] + [(ch(c), sib) for c in (c_p, c_m, c_y, c_2, c_yp, c_ym, c_y2)]

        def start(self, *which):
            ops = self.ops()
            for i in which:
                self.copy(i, *ops[i]).start()

        def wait(self, role):
            self.copy(0, role, sib).wait_recv()

        def first(self):
            self.start(0, 1, 2, 3, 4)

        def relay_near(self):
            self.wait(2 * c_y + core)
            self.start(5, 6, 10)
            self.wait(2 * c_p + core)
            self.start(8)
            self.wait(2 * c_m + core)
            self.start(9)

        def relay_far(self):
            self.wait(2 * c_2 + core)
            self.start(7, 11)

        def late(self):
            for i, c in ((12, c_yp), (13, c_ym), (14, c_y2)):
                self.wait(2 * c + core)
                self.start(i)

        def from_sib(self, c):
            self.wait(2 * c + (1 - core))

        def drain(self):
            ops = self.ops()
            for i in range(15):
                self.copy(i, *ops[i]).wait_send()

    def x_copy(c):
        return pltpu.make_async_copy(
            x_hbm.at[:, pl.ds(pl.multiple_of(c * 2 * KB, 2 * KB), 2 * KB)], xv.at[c], x_sem.at[c]
        )

    w_c = pltpu.make_async_copy(w_hbm, wv.at[me], in_sem.at[0])
    kv_c = pltpu.make_async_copy(kv_hbm, kv, in_sem.at[1])
    dq_c = pltpu.make_async_copy(dq_hbm, dq, in_sem.at[2])
    dkv_c = pltpu.make_async_copy(dkv_hbm, dkv, in_sem.at[3])
    wout_c = pltpu.make_async_copy(wout_hbm, wout, in_sem.at[4])
    w_c.start()
    dq_c.start()
    dkv_c.start()
    kv_c.start()

    barrier = pltpu.get_barrier_semaphore()

    def greet_role(d, _):
        pl.semaphore_signal(barrier, inc=1, device_id=((me + d) % NR, tp), device_id_type=MESH)
        return 0

    lax.fori_loop(1, NR, greet_role, 0)
    for d in (1, 3):
        pl.semaphore_signal(barrier, inc=1, device_id=(me, 4 * yl + (xx + d) % 4), device_id_type=MESH)
    pl.semaphore_signal(barrier, inc=1, device_id=(me, 4 * (1 - yl) + xx), device_id_type=MESH)

    chips = [chip_at(i % 4, i // 4) for i in range(8)]
    for c in chips:
        x_copy(c).start()
    wout_c.start()

    lane = lax.broadcasted_iota(jnp.int32, (8, 128), 1)
    owners = [owner_ref[0, i] for i in range(NP)]
    tags = jnp.full((8, 128), -1, jnp.int32)
    slots = []
    for i in range(NP):
        rank = jnp.int32(0)
        for j in range(i):
            rank = rank + (owners[j] == owners[i]).astype(jnp.int32)
        slot = 2 * owners[i] + rank
        slots.append(slot)
        slot_of[i] = slot
        tags = jnp.where(lane == slot, req_ref[i], tags)
    vtag[...] = tags
    rtag[me] = tags

    sq[...] = jnp.zeros_like(sq)

    def squares(i, _):
        c = chip_at(i % 4, i // 4)
        x_copy(c).wait()

        def tile(t, _):
            rows = pl.ds(pl.multiple_of(t * SQ_TILE, SQ_TILE), SQ_TILE)
            part = sq[rows, :]
            for j in range(2 * KB // 128):
                xf = xv[c, rows, j * 128 : j * 128 + 128].astype(F32)
                part = part + xf * xf
            sq[rows, :] = part
            return 0

        lax.fori_loop(0, ROWS // SQ_TILE, tile, 0)
        return 0

    w_c.wait()

    pl.semaphore_wait(barrier, NR - 1 + 3)

    def send_tag(d, _):
        p = (me + d) % NR
        rc(vtag, rtag.at[me], tag_ss.at[d], tag_rs.at[me], p).start()
        return 0

    lax.fori_loop(1, NR, send_tag, 0)
    w_all = Gather(lambda r: wv.at[r], lambda i: w_ss.at[i], lambda r: w_rs.at[r])
    w_all.first()

    dq_c.wait()
    for s in range(STEPS):
        for h in range(PER):
            qf[pl.ds(s * PER + h, RQ, stride=RQ), :] = dq[s, :, h * HS : (h + 1) * HS].astype(F32)

    def by_request(r, _):
        qb[r] = qf[pl.ds(pl.multiple_of(r * RQ, RQ), RQ), :].astype(BF)
        return 0

    lax.fori_loop(0, RQ, by_request, 0, unroll=4)

    def find_page(s, _):
        i = jnp.int32(0)
        for j in range(NP):
            i = jnp.where(slots[j] == s, j, i)
        page_of[s] = i
        return 0

    lax.fori_loop(0, 2 * NR, find_page, 0)

    acc[...] = jnp.zeros_like(acc)
    lax.fori_loop(0, 8, squares, 0)

    def invert(t, _):
        rows = pl.ds(pl.multiple_of(t * PAGE, PAGE), PAGE)
        mean = jnp.sum(sq[rows, :], axis=1, keepdims=True) * (1.0 / (NR * KB))
        sq[rows, :] = jnp.broadcast_to(lax.rsqrt(mean + EPSILON), (PAGE, 128))
        return 0

    lax.fori_loop(0, NP, invert, 0)

    dkv_c.wait()
    kv_c.wait()

    def attend(r, _):
        q = qb[r]
        pages = [kv[bt_ref[j, r]] for j in range(4)]
        own = dkv[...]
        keys = jnp.concatenate([p[:, :HS] for p in pages], axis=0)
        values = jnp.concatenate([p[:, HS:] for p in pages], axis=0)
        s1 = lax.dot_general(q, keys, NT_DIMS, preferred_element_type=F32) * SCALING
        s2 = lax.dot_general(q, own[:, :HS], NT_DIMS, preferred_element_type=F32) * SCALING
        col = lax.broadcasted_iota(jnp.int32, s1.shape, 1)
        s1 = jnp.where(col < len_ref[r], s1, LOW)
        col2 = lax.broadcasted_iota(jnp.int32, s2.shape, 1)
        row2 = lax.broadcasted_iota(jnp.int32, s2.shape, 0)
        s2 = jnp.where((col2 % RQ == r) & (col2 // RQ <= row2 // PER), s2, LOW)
        top = jnp.maximum(jnp.max(s1, axis=1, keepdims=True), jnp.max(s2, axis=1, keepdims=True))
        p1 = jnp.exp(s1 - top)
        p2 = jnp.exp(s2 - top)
        total = jnp.sum(p1, axis=1, keepdims=True) + jnp.sum(p2, axis=1, keepdims=True)
        o = jnp.dot(p1.astype(BF), values, preferred_element_type=F32)
        o = o + jnp.dot(p2.astype(BF), own[:, HS:], preferred_element_type=F32)
        ac[pl.ds(r, RQ, stride=RQ), :] = o / total
        lc[pl.ds(r, RQ, stride=RQ), :] = jnp.broadcast_to(top + jnp.log(total), (RQ, HS))
        return 0

    def ask():
        tmat = jnp.full((8, 128), -1, jnp.int32)

        def wait_tag(d, t):
            p = (me - d + NR) % NR

            @pl.when(d > 0)
            def _():
                rc(vtag, rtag.at[p], tag_ss.at[0], tag_rs.at[p], p).wait_recv()

            moved = pltpu.roll(rtag[p], (2 * p - 2 * me + 128) % 128, 1)
            return jnp.where(lane // 2 == p, moved, t)

        tmat = lax.fori_loop(0, NR, wait_tag, tmat)
        tvec[...] = tmat
        t_c = pltpu.make_async_copy(tvec, tsm, t_sem)
        t_c.start()
        t_c.wait()

        def pick(s, _):
            qs[s] = qb[jnp.maximum(tsm[0, s], 0)]
            return 0

        lax.fori_loop(0, 2 * NR, pick, 0, unroll=4)

        def send_q(d, _):
            p = (me + d) % NR
            rc(qs.at[pl.ds(2 * p, 2)], qr.at[pl.ds(2 * me, 2)], q_ss.at[d], q_rs.at[me], p).start()
            return 0

        lax.fori_loop(1, NR, send_q, 0)
        qr[pl.ds(2 * me, 2)] = qs[pl.ds(2 * me, 2)]

    def project(c):
        def tile(t, _):
            rows = pl.ds(pl.multiple_of(t * TILE, TILE), TILE)
            inverse = sq[rows, :]
            normed = []
            for j in range(2 * KB // 128):
                gain = gain_ref[2 * c + j // 4, j % 4 : j % 4 + 1, :].astype(F32)
                xf = xv[c, rows, j * 128 : j * 128 + 128].astype(F32)
                normed.append((xf * inverse * gain).astype(BF))
            normed = jnp.concatenate(normed, axis=1)
            acc[rows, :] += jnp.dot(normed, wv[pl.ds(2 * c, 2)].reshape(2 * KB, KVW), preferred_element_type=F32)
            return 0

        lax.fori_loop(0, ROWS // TILE, tile, 0)

    def group(i, _):
        lax.fori_loop(0, 8, lambda r, carry: attend(8 * i + r, carry), 0, unroll=UNROLL)

        @pl.when(i == 1)
        def _():
            ask()
            w_all.relay_near()

        @pl.when(i == 2)
        def _():
            w_all.wait(sib)
            project(chip)
            w_all.relay_far()

        return 0

    lax.fori_loop(0, RQ // 8, group, 0)

    def next_chip(i, _):
        c = chip_at(i % 4, i // 4)
        w_all.from_sib(c)
        project(c)
        return 0

    lax.fori_loop(1, 5, next_chip, 0)
    w_all.late()
    lax.fori_loop(5, 8, next_chip, 0)

    def wait_q(d, _):
        p = (me - d + NR) % NR
        rc(qs.at[pl.ds(0, 2)], qr.at[pl.ds(2 * p, 2)], q_ss.at[0], q_rs.at[p], p).wait_recv()
        return 0

    lax.fori_loop(1, NR, wait_q, 0)
    bias = bias_ref[...].astype(F32)
    bias = jnp.concatenate([bias[0:1], bias[1:2]], axis=1)
    lane_k = lax.broadcasted_iota(jnp.int32, (RQ, 128), 1)

    def page(i, st):
        rows = pl.ds(pl.multiple_of(i * PAGE, PAGE), PAGE)
        f = (acc[rows, :] + bias).astype(BF)
        slot = slot_of[i]
        q = qr[slot]
        s = lax.dot_general(q, f[:, :HS], NT_DIMS, preferred_element_type=F32) * SCALING
        top = jnp.max(s, axis=1, keepdims=True)
        p = jnp.exp(s - top)
        total = jnp.sum(p, axis=1, keepdims=True)
        o = jnp.dot(p.astype(BF), f[:, HS:], preferred_element_type=F32) / total
        pacc[i] = o.astype(BF)
        return jnp.where(lane_k == slot, top + jnp.log(total), st)

    st = lax.fori_loop(0, NP, page, jnp.full((RQ, 128), LOW, F32), unroll=True)
    packed = st[0:8]
    for a in range(1, 4):
        packed = jnp.where(lane // 32 == a, pltpu.roll(st[8 * a : 8 * a + 8], 32 * a, 1), packed)
    sst[...] = packed
    rst[me] = packed

    def place(s, _):
        accs[s] = pacc[page_of[s]]
        return 0

    lax.fori_loop(0, 2 * NR, place, 0, unroll=4)

    def send_acc(d, _):
        p = (me + d) % NR
        rc(accs.at[pl.ds(2 * p, 2)], racc.at[pl.ds(2 * me, 2)], a_ss.at[d], a_rs.at[me], p).start()
        rc(sst, rst.at[me], l_ss.at[d], l_rs.at[me], p).start()
        return 0

    lax.fori_loop(1, NR, send_acc, 0)
    racc[pl.ds(2 * me, 2)] = accs[pl.ds(2 * me, 2)]

    lt[...] = jnp.full((RQ, 128), LOW, F32)

    def wait_acc(d, _):
        p = (me - d + NR) % NR
        rc(sst, rst.at[p], l_ss.at[0], l_rs.at[p], p).wait_recv()
        rc(accs.at[pl.ds(0, 2)], racc.at[pl.ds(2 * p, 2)], a_ss.at[0], a_rs.at[p], p).wait_recv()
        return 0

    lax.fori_loop(1, NR, wait_acc, 0)

    def take(p, _):
        got = rst[p]
        for a in range(4):
            moved = pltpu.roll(got, (2 * p - 2 * me - 32 * a + 256) % 128, 1)
            lt[8 * a : 8 * a + 8, :] = jnp.where(lane // 2 == p, moved, lt[8 * a : 8 * a + 8, :])
        for c in range(2):
            sb[pl.ds(2 * p + c, RQ, stride=RQ), :] = racc[2 * p + c].astype(F32)
        return 0

    lax.fori_loop(0, NR, take, 0, unroll=4)

    mine = jnp.broadcast_to(tvec[0:1, :], (RQ, 128)) == lax.broadcasted_iota(jnp.int32, (RQ, 128), 0)

    def outputs(s):
        return Gather(lambda r: aall.at[s, r], lambda i: g_ss.at[s, i], lambda r: g_rs.at[s, r])

    def merge(s):
        for h in range(PER):
            k = s * PER + h
            rows = pl.ds(pl.multiple_of(k * RQ, RQ), RQ)
            scores = jnp.where(mine, jnp.broadcast_to(lt[pl.ds(k, 1), :], (RQ, 128)), LOW)
            base = lc[rows, :]
            top = jnp.maximum(jnp.max(scores, axis=1, keepdims=True), base)
            e = jnp.exp(scores - top)
            wc = jnp.exp(base - top)
            total = wc + jnp.sum(e, axis=1, keepdims=True)
            pv = jnp.dot(e[:, : 2 * NR].astype(BF), sb[rows, :].astype(BF), preferred_element_type=F32)
            merged = (wc * ac[rows, :] + pv) / total
            aall[s, me, :, h * HS : (h + 1) * HS] = merged.astype(BF)
        outputs(s).first()

    x_p, x_m, x_2 = (xx + 1) % 4, (xx + 3) % 4, (xx + 2) % 4

    def x_send(s, i):
        to = x_m if i % 2 else x_p
        src, dst = (
            (ps.at[s, x_2, 0], pa.at[s, 0]),
            (ps.at[s, x_2, 1], pa.at[s, 1]),
            (ps.at[s, x_p, 1], px.at[s, 0, 1]),
            (ps.at[s, x_m, 0], px.at[s, 1, 0]),
            (ps.at[s, x_p, 0], px.at[s, 0, 0]),
            (ps.at[s, x_m, 1], px.at[s, 1, 1]),
        )[i]
        return rc(src, dst, p_ss.at[s, i], p_rs.at[s, i], me, 4 * yl + to)

    def relay_x(s):
        x_send(s, 0).wait_recv()
        ps[s, x_p, 0] = (ps[s, x_p, 0].astype(F32) + pa[s, 0].astype(F32)).astype(BF)
        x_send(s, 4).start()
        x_send(s, 1).wait_recv()
        ps[s, x_m, 1] = (ps[s, x_m, 1].astype(F32) + pa[s, 1].astype(F32)).astype(BF)
        x_send(s, 5).start()

    def y_send(s):
        return rc(ys.at[s], py.at[s], y_ss.at[s], y_rs.at[s], me, 4 * (1 - yl) + xx)

    def product(s):
        g = outputs(s)
        g.late()
        g.wait(sib)
        for c in chips[1:]:
            g.from_sib(c)

        def part(j, _):
            a = aall[s, pl.ds(j * 8, 8)].reshape(8 * RQ, 1024)
            o = jnp.dot(a, wout[...], preferred_element_type=F32).astype(BF)
            o = o.reshape(4, 2 * RQ, NOUT)
            for i in range(4):
                for h in range(2):
                    ps[s, i, h, j] = o[i, :, h * 256 : h * 256 + 256]
            return 0

        lax.fori_loop(0, 2, part, 0)
        for i in range(4):
            x_send(s, i).start()

    def add_x(s):
        for i in range(2, 6):
            x_send(s, i).wait_recv()
        for half in range(2):
            o = jnp.concatenate(
                [
                    ps[s, xx, h, half].astype(F32) + px[s, 0, h, half].astype(F32) + px[s, 1, h, half].astype(F32)
                    for h in range(2)
                ],
                axis=1,
            )

            @pl.when(yl == half)
            def _():
                ko[s] = o

            @pl.when(yl != half)
            def _():
                ys[s] = o.astype(BF)

        y_send(s).start()

    def add_y(s):
        y_send(s).wait_recv()
        out_ref[s] = (ko[s] + py[s].astype(F32)).astype(BF)

    merge(0)
    merge(1)
    wout_c.wait()

    def round_(i, _):
        @pl.when(i < STEPS)
        def _():
            outputs(i).relay_near()
            outputs(i).relay_far()

        @pl.when(i < STEPS - 2)
        def _():
            merge(i + 2)

        @pl.when((i >= 1) & (i <= STEPS))
        def _():
            product(i - 1)

        @pl.when((i >= 3) & (i <= STEPS + 2))
        def _():
            add_x(i - 3)

        @pl.when(i >= 4)
        def _():
            add_y(i - 4)

        @pl.when((i >= 2) & (i <= STEPS + 1))
        def _():
            relay_x(i - 2)

        return 0

    lax.fori_loop(0, STEPS + 4, round_, 0)

    def drain(d, _):
        rc(vtag, rtag.at[me], tag_ss.at[d], tag_rs.at[me], sib).wait_send()
        rc(qs.at[pl.ds(0, 2)], qr.at[pl.ds(0, 2)], q_ss.at[d], q_rs.at[me], sib).wait_send()
        rc(accs.at[pl.ds(0, 2)], racc.at[pl.ds(0, 2)], a_ss.at[d], a_rs.at[me], sib).wait_send()
        rc(sst, rst.at[me], l_ss.at[d], l_rs.at[me], sib).wait_send()
        return 0

    lax.fori_loop(1, NR, drain, 0)
    w_all.drain()

    def drain_s(s, _):
        outputs(s).drain()
        for i in range(6):
            x_send(s, i).wait_send()
        y_send(s).wait_send()
        return 0

    lax.fori_loop(0, STEPS, drain_s, 0)


def body(
    x_pre,
    ln_gain,
    w_kv,
    kv_bias,
    page_owner,
    page_req,
    kv_pool,
    block_table,
    cache_len,
    dec_q,
    dec_kv,
    w_out,
):
    any_spec = pl.BlockSpec(memory_space=pl.ANY)
    smem = pl.BlockSpec(memory_space=pltpu.SMEM)
    vmem = pl.BlockSpec(memory_space=pltpu.VMEM)
    dma = pltpu.SemaphoreType.DMA
    V = pltpu.VMEM
    scratch = [
        V((8, ROWS, 2 * KB), BF),
        V((NR, KB, KVW), BF),
        V((32, PAGE, KVW), BF),
        V((STEPS, RQ, 1024), BF),
        V((STEPS * RQ, KVW), BF),
        V((1024, NOUT), BF),
        V((ROWS, KVW), F32),
        V((ROWS, 128), F32),
        V((RQ * RQ, HS), F32),
        V((RQ, RQ, HS), BF),
        V((RQ * RQ, HS), F32),
        V((RQ * RQ, HS), F32),
        V((8, 128), jnp.int32),
        V((NR, 8, 128), jnp.int32),
        V((8, 128), jnp.int32),
        pltpu.SMEM((8, 128), jnp.int32),
        pltpu.SMEM((16,), jnp.int32),
        pltpu.SMEM((2 * NR,), jnp.int32),
        V((2 * NR, RQ, HS), BF),
        V((2 * NR, RQ, HS), BF),
        V((NP, RQ, HS), BF),
        V((2 * NR, RQ, HS), BF),
        V((2 * NR, RQ, HS), BF),
        V((8, 128), F32),
        V((NR, 8, 128), F32),
        V((RQ, 128), F32),
        V((RQ * RQ, HS), F32),
        V((STEPS, NR, RQ, 1024), BF),
        V((STEPS, 4, 2, 2, 2 * RQ, 256), BF),
        V((STEPS, 2, 2, 2 * RQ, 256), BF),
        V((STEPS, 2, 2, 2, 2 * RQ, 256), BF),
        V((STEPS, 2 * RQ, NOUT), BF),
        V((STEPS, 2 * RQ, NOUT), BF),
        V((STEPS, 2 * RQ, NOUT), F32),
        dma((8,)),
        dma((5,)),
        dma,
        dma((15,)),
        dma((NR,)),
        dma((NR,)),
        dma((NR,)),
        dma((NR,)),
        dma((NR,)),
        dma((NR,)),
        dma((NR,)),
        dma((NR,)),
        dma((NR,)),
        dma((STEPS, 15)),
        dma((STEPS, NR)),
        dma((STEPS, 6)),
        dma((STEPS, 6)),
        dma((STEPS,)),
        dma((STEPS,)),
    ]
    return pl.pallas_call(
        kernel,
        out_shape=jax.ShapeDtypeStruct((STEPS, 2 * RQ, NOUT), BF),
        in_specs=[any_spec, vmem, any_spec, vmem, smem, smem, any_spec, smem, smem, any_spec, any_spec, any_spec],
        out_specs=vmem,
        scratch_shapes=scratch,
        compiler_params=pltpu.CompilerParams(
            collective_id=0, has_side_effects=True, vmem_limit_bytes=58 * 1024 * 1024
        ),
    )(
        x_pre,
        ln_gain.reshape(NR, KB // 128, 128),
        w_kv,
        kv_bias.reshape(2, HS),
        page_owner.T,
        page_req,
        kv_pool,
        block_table.T,
        cache_len,
        dec_q,
        dec_kv.reshape(STEPS * RQ, KVW),
        w_out,
    )


def solution(mesh):
    return jax.shard_map(
        body,
        mesh=mesh,
        in_specs=(
            P("role", None),
            P(),
            P("role", "tp"),
            P("tp"),
            P("role", None),
            P("role"),
            P("role", None, "tp"),
            P("role", None),
            P("role"),
            P(None, "role", "tp"),
            P(None, "role", "tp"),
            P("tp", "role"),
        ),
        out_specs=P(None, "tp", "role"),
        check_vma=False,
    )
```
